256 devices in a mesh: seq: 16 (over z_lo, y), head: 16 (over x, z_hi, core).
Axes of the slice: x: 4, y: 4, z: 8 (z_hi: 2, z_lo: 4; z = z_hi * 4 + z_lo), core: 2. Of those that a mesh axis runs over, the one named last changes fastest.
Arguments:
- queries: bfloat16 [8192, 4096], P('seq', 'head'), may hold values from -60 to 60
- keys: bfloat16 [8192, 4096], P('seq', 'head'), may hold values from -60 to 60
- values: bfloat16 [8192, 4096], P('seq', 'head'), may hold values from -6 to 6
- w_out: bfloat16 [4096, 4096], P('head'), may hold values from -0.125 to 0.125
- d_mixed: bfloat16 [8192, 4096], P('seq', 'head'), may hold values from -6 to 6
- random_blocks: int32 [64, 3], P('seq'), may hold values from 0 to 63, as said below
- global_blocks: int32 [2], replicated, may hold values from 0 to 63, as said below
Outputs:
- mixed: bfloat16 [8192, 4096], P('seq', 'head')
- query_grad: bfloat16 [8192, 4096], P('seq', 'head')
- key_grad: bfloat16 [8192, 4096], P('seq', 'head')
- value_grad: bfloat16 [8192, 4096], P('seq', 'head')
The draws below stay inside these ranges and needn't reach their ends.
Inputs may be any that keep to these rules, and one draw needn't show every extreme that they name: `random_blocks`: blocks b * 4 to (b + 1) * 4 - 1 lie on index b of seq. The random blocks named by the 4 query blocks of one index of seq include at most 2 distinct blocks of any one index of seq, and exactly 2 for some. `global_blocks`: the 2 global blocks are distinct; the document's last block is always one of them.
All inputs are finite; a program needn't handle non-finite values.
Results may differ from the reference program's by a relative error of at most 0.033.
Values may be sent and summed in bfloat16 or wider, within the bound.
A program may use at most 128 MiB of HBM per device.

```python
import jax
import jax.numpy as jnp
from jax import lax

HEADS = 32
HEAD_DIM = 128
BLOCK = 128
RANDOM = 3
GLOBALS = 2
D = 4096
BLOCKS_DEV = 4
NBLOCKS = 64
TOKENS = 8192


def drawn_pair(key):
    base_key = jax.random.fold_in(key, 7)
    key_query, key_key = jax.random.split(base_key, 2)
    query_draw = jnp.clip(jax.random.normal(key_query, (TOKENS, D), jnp.float32), -5.0, 5.0)
    key_draw = jnp.clip(jax.random.normal(key_key, (TOKENS, D), jnp.float32), -5.0, 5.0)
    return (query_draw, key_draw)


def draw_queries(key, part):
    return drawn_pair(key)[0].astype(jnp.bfloat16)


def draw_keys(key, part):
    return drawn_pair(key)[1].astype(jnp.bfloat16)


def draw_random_blocks(key, part):
    holders = NBLOCKS // BLOCKS_DEV
    per_device = BLOCKS_DEV * RANDOM
    pair_count = per_device // 2
    key_order, key_first, key_step = jax.random.split(jax.random.fold_in(key, 11), 3)
    order_scores = jax.random.randint(key_order, (holders, holders), 0, 1 << 20) * holders + jnp.arange(holders, dtype=jnp.int32)[None, :]
    owners = jnp.argsort(order_scores, axis=1)[:, :pair_count].astype(jnp.int32)
    first = jax.random.randint(key_first, (holders, pair_count), 0, BLOCKS_DEV)
    offset = jax.random.randint(key_step, (holders, pair_count), 1, BLOCKS_DEV)
    second = (first + offset) % BLOCKS_DEV
    local = jnp.stack([first, second], axis=2).reshape(holders, per_device)
    owner_slots = jnp.repeat(owners, 2, axis=1)
    block_ids = owner_slots * BLOCKS_DEV + local
    return block_ids.reshape(NBLOCKS, RANDOM).astype(jnp.int32)


def draw_global_blocks(key, part):
    key = jax.random.fold_in(key, 13)
    key_pick, key_place = jax.random.split(key, 2)
    order_scores = jax.random.randint(key_pick, (NBLOCKS - 1,), 0, 1 << 20) * NBLOCKS + jnp.arange(NBLOCKS - 1, dtype=jnp.int32)
    others = jnp.argsort(order_scores)[:GLOBALS - 1].astype(jnp.int32)
    chosen = jnp.concatenate([others, jnp.full((1,), NBLOCKS - 1, jnp.int32)])
    return jax.random.permutation(key_place, chosen).astype(jnp.int32)


def with_spikes(entries, rng, source, target, shards_of, factor):
    owner, partner = [(jnp.arange(entries.shape[dim]) // (entries.shape[dim] // shards_of)).reshape([-1 if axis == dim else 1 for axis in range(entries.ndim)]) for dim in (source, target)]
    chosen = jax.random.permutation(rng, shards_of)[partner]
    strong = (owner == chosen) | (owner == (partner + shards_of // 2) % shards_of)
    return jnp.where(strong, factor * entries, entries)


def block_scale(stream_key, extent, cuts, low, largest):
    def one(dim, blocks):
        heights = jax.random.uniform(jax.random.fold_in(jax.random.fold_in(stream_key, 6), dim), (blocks,), jnp.float32, low / len(cuts), largest / len(cuts))
        return jnp.repeat(jnp.exp(heights), extent[dim] // blocks).reshape((-1,) + (1,) * (len(extent) - dim - 1))

    loudness = one(*cuts[0])
    for cut in cuts[1:]:
        loudness = loudness * one(*cut)
    return loudness


def noise(stream_key, shape, width, most, cuts=(), held_as=jnp.bfloat16):
    values = width * jax.random.normal(stream_key, shape, jnp.float32)
    if cuts:
        values = values * block_scale(stream_key, shape, cuts, -0.22, 0.18)
    return jnp.clip(values, -most, most).astype(held_as)


def heavy_noise(rng, shape, deviation, limit, cuts, heavy, kind=jnp.bfloat16):
    values = deviation * jax.random.normal(rng, shape, jnp.float32)
    if cuts:
        values = values * block_scale(rng, shape, cuts, -0.22, 0.18)
    return jnp.clip(with_spikes(values, jax.random.fold_in(rng, 3), *heavy), -limit, limit).astype(kind)


def setup_inputs(seed: int = 0) -> dict:
    streams_of = jax.random.split(jax.random.key(seed), 8)
    queries = draw_queries(jax.random.fold_in(streams_of[7], 71), 0)
    keys = draw_keys(jax.random.fold_in(streams_of[7], 71), 0)
    values = noise(streams_of[2], (TOKENS, D), 1.0, 6.0, ((0, 16), (1, 16)))
    w_out = heavy_noise(streams_of[3], (D, D), D ** -0.5, 0.125, ((0, 16),), (0, 1, 16, 2.0))
    d_mixed = noise(streams_of[4], (TOKENS, D), 1.0, 6.0, ((0, 16), (1, 16)))
    random_blocks = draw_random_blocks(jax.random.fold_in(streams_of[7], 71), 0)
    global_blocks = draw_global_blocks(jax.random.fold_in(streams_of[7], 71), 0)
    return dict(queries=queries, keys=keys, values=values, w_out=w_out, d_mixed=d_mixed, random_blocks=random_blocks, global_blocks=global_blocks)


def slot_table(first_ids, block_count, random_rows, global_blocks):
    band_ids = first_ids[:, None] + jnp.arange(-1, 2, dtype=jnp.int32)[None, :]
    global_ids = jnp.broadcast_to(global_blocks[None, :], (first_ids.shape[0], global_blocks.shape[0]))
    slot_ids = jnp.concatenate([band_ids, random_rows, global_ids], axis=1).astype(jnp.int32)
    inside = (slot_ids >= 0) & (slot_ids < block_count)
    slot_count = slot_ids.shape[1]
    same_block = slot_ids[:, :, None] == slot_ids[:, None, :]
    earlier = jnp.arange(slot_count)[None, :] < jnp.arange(slot_count)[:, None]
    repeated = jnp.any(same_block & earlier[None, :, :], axis=2)
    return slot_ids, inside & jnp.logical_not(repeated)


def reference(queries, keys, values, w_out, d_mixed, random_blocks, global_blocks):
    score_scale = HEAD_DIM ** -0.5
    block_count = NBLOCKS
    slot_ids, slot_live = slot_table(jnp.arange(block_count, dtype=jnp.int32), block_count, random_blocks, global_blocks)
    safe_ids = jnp.clip(slot_ids, 0, block_count - 1)
    slot_count = slot_ids.shape[1]
    query_all = queries.reshape(block_count, BLOCK, HEADS, HEAD_DIM)
    key_all = keys.reshape(block_count, BLOCK, HEADS, HEAD_DIM)
    value_all = values.reshape(block_count, BLOCK, HEADS, HEAD_DIM)

    def scores(block_index):
        query_block = query_all[block_index].astype(jnp.float32)
        key_rows = key_all[safe_ids[block_index]].reshape(slot_count * BLOCK, HEADS, HEAD_DIM).astype(jnp.float32)
        value_rows = value_all[safe_ids[block_index]].reshape(slot_count * BLOCK, HEADS, HEAD_DIM).astype(jnp.float32)
        row_mask = jnp.repeat(slot_live[block_index], BLOCK)
        logits = jnp.einsum('ihd,khd->hik', query_block, key_rows) * score_scale
        logits = jnp.where(row_mask[None, None, :], logits, -1e30)
        return query_block, key_rows, value_rows, logits

    def forward(block_index):
        query_block, key_rows, value_rows, logits = scores(block_index)
        row_max = jnp.max(logits, axis=-1, keepdims=True)
        log_total = row_max + jnp.log(jnp.sum(jnp.exp(logits - row_max), axis=-1, keepdims=True))
        prob_half = jnp.exp(logits - log_total).astype(jnp.bfloat16)
        output = jnp.einsum('hik,khd->ihd', prob_half.astype(jnp.float32), value_rows).astype(jnp.bfloat16)
        return output, log_total[..., 0]

    attn_blocks, totals_all = lax.map(forward, jnp.arange(block_count, dtype=jnp.int32))
    attn = attn_blocks.reshape(TOKENS, D)
    mixed = jnp.dot(attn, w_out, preferred_element_type=jnp.float32).astype(jnp.bfloat16)
    d_attn = jnp.dot(d_mixed, w_out.T, preferred_element_type=jnp.float32).astype(jnp.bfloat16)
    delta_all = jnp.sum((attn.astype(jnp.float32) * d_attn.astype(jnp.float32)).reshape(block_count, BLOCK, HEADS, HEAD_DIM), axis=-1)
    grad_all = d_attn.reshape(block_count, BLOCK, HEADS, HEAD_DIM)

    def backward(carry, block_index):
        key_sum, value_sum = carry
        query_block, key_rows, value_rows, logits = scores(block_index)
        prob_full = jnp.exp(logits - totals_all[block_index][..., None])
        prob_half = prob_full.astype(jnp.bfloat16)
        grad_block = grad_all[block_index].astype(jnp.float32)
        prob_grad = jnp.einsum('ihd,khd->hik', grad_block, value_rows)
        score_grad = (prob_full * (prob_grad - jnp.transpose(delta_all[block_index])[..., None]) * score_scale).astype(jnp.bfloat16)
        query_part = jnp.einsum('hik,khd->ihd', score_grad.astype(jnp.float32), key_rows).astype(jnp.bfloat16)
        key_part = jnp.einsum('hik,ihd->khd', score_grad.astype(jnp.float32), query_block).reshape(slot_count, BLOCK, HEADS, HEAD_DIM)
        value_part = jnp.einsum('hik,ihd->khd', prob_half.astype(jnp.float32), grad_block).reshape(slot_count, BLOCK, HEADS, HEAD_DIM)
        key_sum = key_sum.at[safe_ids[block_index]].add(key_part)
        value_sum = value_sum.at[safe_ids[block_index]].add(value_part)
        return (key_sum, value_sum), query_part

    zero_sums = jnp.zeros((block_count, BLOCK, HEADS, HEAD_DIM), jnp.float32)
    (key_sum, value_sum), query_parts = lax.scan(backward, (zero_sums, zero_sums), jnp.arange(block_count, dtype=jnp.int32))
    query_grad = query_parts.reshape(TOKENS, D)
    key_grad = key_sum.reshape(TOKENS, D).astype(jnp.bfloat16)
    value_grad = value_sum.reshape(TOKENS, D).astype(jnp.bfloat16)
    return (mixed, query_grad, key_grad, value_grad)
```

```python
import jax
import jax.numpy as jnp
from jax import lax
from jax.experimental import pallas as pl
from jax.experimental.pallas import tpu as pltpu
from jax.sharding import PartitionSpec as P

HEAD_DIM = 128
BLOCK = 128
SLOTS = 8
MASKED = -1e30
MESH = pl.DeviceIdType.MESH
BF16 = jnp.bfloat16
F32 = jnp.float32
VMEM_LIMIT = 56 * 1024 * 1024


def place():
    seq, head = lax.axis_index("seq"), lax.axis_index("head")
    return seq // 4, seq % 4, head // 4, (head // 2) % 2, head % 2


def dev(z, y, x, zh, core):
    return (z * 4 + y, x * 4 + zh * 2 + core)


def copy_to(src, dst, send_sem, recv_sem, device):
    return pltpu.make_async_remote_copy(
        src_ref=src,
        dst_ref=dst,
        send_sem=send_sem,
        recv_sem=recv_sem,
        device_id=device,
        device_id_type=MESH,
    )


def greet():
    z, y, x, zh, core = place()
    barrier = pltpu.get_barrier_semaphore()
    others = [dev(z, y, x, zh, 1 - core)]
    for step in (1, 2, 3):
        for r in (0, 1):
            others.append(dev((z + step) % 4, y, x, zh, r))
    others += [dev(z, (y + 1) % 4, x, zh, core), dev(z, (y + 3) % 4, x, zh, core)]
    others += [dev(z, y, (x + 1) % 4, zh, core), dev(z, y, (x + 3) % 4, zh, core)]
    others.append(dev(z, y, x, 1 - zh, core))
    for other in others:
        pl.semaphore_signal(barrier, inc=1, device_id=other, device_id_type=MESH)
    pl.semaphore_wait(barrier, len(others))


def gather_kernel(
    q_ref,
    k_ref,
    v_ref,
    dm_ref,
    w_ref,
    rb_ref,
    kv_ref,
    qm_ref,
    da_ref,
    rbm_ref,
    dm_all,
    grad,
    grad_acc,
    a_send,
    a_recv,
    b_send,
    b_recv,
    y_send,
    y_recv,
    ys_send,
    ys_recv,
    z_send,
    z_recv,
    x_send,
    x_recv,
    xs_send,
    xs_recv,
    g_send,
    g_recv,
):
    z, y, x, zh, core = place()
    sibling = dev(z, y, x, zh, 1 - core)
    sent = []
    greet()

    def send(src, dst, send_sem, recv_sem, device):
        copy = copy_to(src, dst, send_sem, recv_sem, device)
        copy.start()
        sent.append(copy)

    def arrive(dst, recv_sem, send_sem):
        copy_to(dst, dst, send_sem, recv_sem, sibling).wait_recv()

    y_up, y_down = dev(z, (y + 1) % 4, x, zh, core), dev(z, (y + 3) % 4, x, zh, core)
    x_up, x_down = dev(z, y, (x + 1) % 4, zh, core), dev(z, y, (x + 3) % 4, zh, core)
    y_of = {0: y, 1: (y + 3) % 4, 2: (y + 1) % 4, 3: (y + 2) % 4}
    x_of = {0: x, 1: (x + 3) % 4, 2: (x + 1) % 4, 3: (x + 2) % 4}

    own_dm = dm_all.at[core, x, zh]
    send(dm_ref, own_dm, z_send.at[0], z_recv.at[0], dev(z, y, x, 1 - zh, core))

    def to_line(src, dst, send_sem, recv_sem, j, r):
        there = 2 * core + j
        here = jnp.logical_and(there == z, core == r)

        @pl.when(here)
        def _():
            pltpu.make_async_copy(src, dst, recv_sem).start()

        @pl.when(jnp.logical_not(here))
        def _():
            copy_to(src, dst, send_sem, recv_sem, dev(there, y, x, zh, r)).start()

    def line_sent(src, dst, send_sem, recv_sem, j, r):
        there = 2 * core + j
        here = jnp.logical_and(there == z, core == r)

        @pl.when(jnp.logical_not(here))
        def _():
            copy_to(src, dst, send_sem, recv_sem, dev(there, y, x, zh, r)).wait_send()

    def line_args():
        for j in (0, 1):
            for r in (0, 1):
                rows, cols = pl.ds(r * 256, 256), pl.ds(j * 128, 128)
                for t, src in enumerate((k_ref, v_ref)):
                    yield (
                        src.at[rows, cols],
                        kv_ref.at[y, r, z, t],
                        a_send.at[t, j, r],
                        a_recv.at[t, z],
                        j,
                        r,
                    )
        for j in (0, 1):
            for r in (0, 1):
                rows, cols = pl.ds(r * 256, 256), pl.ds(j * 128, 128)
                yield (
                    q_ref.at[rows, cols],
                    qm_ref.at[z],
                    a_send.at[2, j, r],
                    a_recv.at[2, z],
                    j,
                    r,
                )

    for args in line_args():
        to_line(*args)
    send(dm_ref, own_dm, x_send.at[0, 0], x_recv.at[0, zh], x_up)
    send(dm_ref, own_dm, x_send.at[0, 1], x_recv.at[1, zh], x_down)
    send(dm_ref, own_dm, xs_send.at[0, 0], xs_recv.at[x, zh], sibling)
    for step in (1, 2, 3):
        send(
            rb_ref,
            rbm_ref.at[z],
            b_send.at[step - 1],
            b_recv.at[step - 1],
            dev((z + step) % 4, y, x, zh, core),
        )
    rbm_ref[z] = rb_ref[...]
    dm_all[core, x, zh] = dm_ref[...]

    for zz in range(4):
        for t in (0, 1):
            arrive(kv_ref.at[y, core, zz, t], a_recv.at[t, zz], a_send.at[t, 0, 0])
        piece = kv_ref.at[y, core, zz]
        send(piece, piece, y_send.at[0, zz], y_recv.at[0, zz], y_up)
        send(piece, piece, y_send.at[1, zz], y_recv.at[1, zz], y_down)
        send(piece, piece, ys_send.at[0, zz], ys_recv.at[0, zz], sibling)

    def dm_block(slot, k):
        return dm_all.at[core, x_of[slot], k]

    other_dm = dm_block(0, 1 - zh)
    arrive(other_dm, z_recv.at[0], z_send.at[0])
    send(other_dm, other_dm, x_send.at[1, 0], x_recv.at[0, 1 - zh], x_up)
    send(other_dm, other_dm, x_send.at[1, 1], x_recv.at[1, 1 - zh], x_down)
    send(other_dm, other_dm, xs_send.at[0, 1], xs_recv.at[x, 1 - zh], sibling)

    def kv_step(slot, recv, onward):
        for zz in range(4):
            piece = kv_ref.at[y_of[slot], core, zz]
            arrive(piece, recv(zz), y_send.at[0, zz])
            if zz in onward[0]:
                send(piece, piece, onward[1].at[zz], y_recv.at[2, zz], onward[2])
            send(piece, piece, ys_send.at[slot, zz], ys_recv.at[slot, zz], sibling)

    kv_step(1, lambda zz: y_recv.at[0, zz], ((0, 1), y_send.at[2], y_up))
    kv_step(2, lambda zz: y_recv.at[1, zz], ((2, 3), y_send.at[2], y_down))

    for slot, index, onward, device in ((1, 0, 0, x_up), (2, 1, 1, x_down)):
        for k in (0, 1):
            block = dm_block(slot, k)
            arrive(block, x_recv.at[index, k], x_send.at[0, 0])
            if k == onward:
                send(block, block, x_send.at[2, k], x_recv.at[2, k], device)
            send(block, block, xs_send.at[slot, k], xs_recv.at[x_of[slot], k], sibling)

    kv_step(3, lambda zz: y_recv.at[2, zz], ((), None, None))
    for k in (0, 1):
        block = dm_block(3, k)
        arrive(block, x_recv.at[2, k], x_send.at[0, 0])
        send(block, block, xs_send.at[3, k], xs_recv.at[x_of[3], k], sibling)

    grad_acc[...] = jnp.zeros_like(grad_acc)

    def add_product(from_core):
        def step(i, carry):
            xx, k = i // 2, i % 2
            at = pl.multiple_of((xx * 4 + k * 2 + from_core) * 256, 256)
            grad_acc[...] += lax.dot_general(
                dm_all[from_core, xx, k],
                w_ref[:, pl.ds(at, 256)],
                (((1,), (1,)), ((), ())),
                preferred_element_type=F32,
            )
            return carry

        lax.fori_loop(0, 8, step, 0)

    add_product(core)
    for xx in range(4):
        for k in (0, 1):
            arrive(dm_all.at[1 - core, xx, k], xs_recv.at[xx, k], xs_send.at[0, 0])
    add_product(1 - core)
    grad[...] = grad_acc[...].astype(BF16)

    def grad_args():
        for j in (0, 1):
            for r in (0, 1):
                yield (
                    grad.at[pl.ds(r * 256, 256), pl.ds(j * 128, 128)],
                    da_ref.at[z],
                    g_send.at[j, r],
                    g_recv.at[z],
                    j,
                    r,
                )

    for args in grad_args():
        to_line(*args)

    for slot in range(4):
        for zz in range(4):
            piece = kv_ref.at[y_of[slot], 1 - core, zz]
            arrive(piece, ys_recv.at[slot, zz], ys_send.at[0, zz])
    for zz in range(4):
        arrive(qm_ref.at[zz], a_recv.at[2, zz], a_send.at[2, 0, 0])
    for step in (1, 2, 3):
        arrive(rbm_ref.at[(z - step + 4) % 4], b_recv.at[step - 1], b_send.at[step - 1])
    for zz in range(4):
        arrive(da_ref.at[zz], g_recv.at[zz], g_send.at[0, 0])
    for args in line_args():
        line_sent(*args)
    for args in grad_args():
        line_sent(*args)
    for copy in sent:
        copy.wait_send()


def gather(q, k, v, dm, w, rb):
    vmem = pl.BlockSpec(memory_space=pltpu.VMEM)
    dma = pltpu.SemaphoreType.DMA
    return pl.pallas_call(
        gather_kernel,
        out_shape=(
            jax.ShapeDtypeStruct((4, 2, 4, 2, 256, 128), BF16),
            jax.ShapeDtypeStruct((4, 256, 128), BF16),
            jax.ShapeDtypeStruct((4, 256, 128), BF16),
            jax.ShapeDtypeStruct((4, 8, 128), jnp.int32),
        ),
        in_specs=[vmem] * 6,
        out_specs=(vmem,) * 4,
        scratch_shapes=[
            pltpu.VMEM((2, 4, 2, 512, 256), BF16),
            pltpu.VMEM((512, 256), BF16),
            pltpu.VMEM((512, 256), F32),
            dma((3, 2, 2)),
            dma((3, 4)),
            dma((3,)),
            dma((3,)),
            dma((3, 4)),
            dma((3, 4)),
            dma((4, 4)),
            dma((4, 4)),
            dma((1,)),
            dma((1,)),
            dma((3, 2)),
            dma((3, 2)),
            dma((4, 2)),
            dma((4, 2)),
            dma((2, 2)),
            dma((4,)),
        ],
        compiler_params=pltpu.CompilerParams(
            collective_id=0, has_side_effects=True, vmem_limit_bytes=VMEM_LIMIT
        ),
        name="gather_heads",
    )(q, k, v, dm, w, rb)


def attention_kernel(
    rb_ref, gb_ref, kv_ref, q_ref, da_ref, o_ref, dq_ref, dkv_ref, acc, kcat, vcat
):
    _, y, _, _, core = place()
    scale = HEAD_DIM ** (-0.5)

    def clear(i, carry):
        acc[i] = jnp.zeros((BLOCK, HEAD_DIM), F32)
        return carry

    lax.fori_loop(0, 128, clear, 0, unroll=4)

    def one(n, carry):
        zz, low = n // 2, n % 2
        i = 2 * core + low
        own = (zz * 4 + y) * 4 + i
        ids = [own - 1, own, own + 1]
        ids += [rb_ref[zz, i, t] for t in range(3)]
        ids += [gb_ref[t] for t in range(2)]
        places, biases = [], []
        for t, block in enumerate(ids):
            dead = jnp.logical_or(block < 0, block > 63)
            for earlier in ids[:t]:
                dead = jnp.logical_or(dead, block == earlier)
            block = jnp.clip(block, 0, 63)
            bz, by, bi = block // 16, (block // 4) % 4, block % 4
            places.append(((by * 2 + bi // 2) * 4 + bz) * 4 + bi % 2)
            biases.append(jnp.where(dead, MASKED, 0.0).astype(F32))
        for t, at in enumerate(places):
            kcat[t * BLOCK : (t + 1) * BLOCK, :] = kv_ref[at]
            vcat[t * BLOCK : (t + 1) * BLOCK, :] = kv_ref[at + 2]
        query, grad = q_ref[n], da_ref[n]
        keys, values = kcat[...], vcat[...]
        bias = jnp.concatenate(
            [jnp.full((1, BLOCK), value, F32) for value in biases], axis=1
        )
        contract_last = (((1,), (1,)), ((), ()))
        contract_first = (((0,), (0,)), ((), ()))
        scores = (
            lax.dot_general(query, keys, contract_last, preferred_element_type=F32) * scale
            + bias
        )
        top = jnp.max(scores, axis=1, keepdims=True)
        powers = jnp.exp(scores - top)
        probs = powers * (1.0 / jnp.sum(powers, axis=1, keepdims=True))
        half = probs.astype(BF16)
        out = jnp.dot(half, values, preferred_element_type=F32).astype(BF16)
        o_ref[n] = out
        delta = jnp.sum(out.astype(F32) * grad.astype(F32), axis=1, keepdims=True)
        prob_grad = lax.dot_general(grad, values, contract_last, preferred_element_type=F32)
        score_grad = (probs * (prob_grad - delta) * scale).astype(BF16)
        dq_ref[n] = jnp.dot(score_grad, keys, preferred_element_type=F32).astype(BF16)
        key_add = lax.dot_general(
            score_grad, query, contract_first, preferred_element_type=F32
        )
        value_add = lax.dot_general(half, grad, contract_first, preferred_element_type=F32)
        for t, at in enumerate(places):
            acc[at] += key_add[t * BLOCK : (t + 1) * BLOCK, :]
            acc[at + 2] += value_add[t * BLOCK : (t + 1) * BLOCK, :]
        return carry

    lax.fori_loop(0, 8, one, 0)

    def finish(i, carry):
        dkv_ref[i] = acc[i].astype(BF16)
        return carry

    lax.fori_loop(0, 128, finish, 0, unroll=4)


def attention(rb, gb, kv, q, da):
    vmem = pl.BlockSpec(memory_space=pltpu.VMEM)
    smem = pl.BlockSpec(memory_space=pltpu.SMEM)
    return pl.pallas_call(
        attention_kernel,
        out_shape=(
            jax.ShapeDtypeStruct((8, BLOCK, HEAD_DIM), BF16),
            jax.ShapeDtypeStruct((8, BLOCK, HEAD_DIM), BF16),
            jax.ShapeDtypeStruct((128, BLOCK, HEAD_DIM), BF16),
        ),
        in_specs=[smem, smem, vmem, vmem, vmem],
        out_specs=(vmem,) * 3,
        scratch_shapes=[
            pltpu.VMEM((128, BLOCK, HEAD_DIM), F32),
            pltpu.VMEM((SLOTS * BLOCK, HEAD_DIM), BF16),
            pltpu.VMEM((SLOTS * BLOCK, HEAD_DIM), BF16),
        ],
        compiler_params=pltpu.CompilerParams(vmem_limit_bytes=VMEM_LIMIT),
        name="block_attention",
    )(rb, gb, kv, q, da)


def scatter_kernel(
    o_ref,
    dq_ref,
    p_ref,
    w_ref,
    mixed_ref,
    dqo_ref,
    dko_ref,
    dvo_ref,
    lands,
    attn,
    terms,
    terms_in,
    xa,
    xb,
    xc,
    xd,
    total,
    zb,
    parts,
    parts_in,
    ya,
    yb,
    yc,
    yd,
    final,
    l_send,
    l_recv,
    ps_send,
    ps_recv,
    y_send,
    y_recv,
    xs_send,
    xs_recv,
    x_send,
    x_recv,
    z_send,
    z_recv,
):
    z, y, x, zh, core = place()
    sibling = dev(z, y, x, zh, 1 - core)
    sent = []
    greet()

    def send(src, dst, send_sem, recv_sem, device):
        copy = copy_to(src, dst, send_sem, recv_sem, device)
        copy.start()
        sent.append(copy)

    def arrive(dst, recv_sem, send_sem):
        copy_to(dst, dst, send_sem, recv_sem, sibling).wait_recv()

    y_up, y_down = dev(z, (y + 1) % 4, x, zh, core), dev(z, (y + 3) % 4, x, zh, core)
    x_up, x_down = dev(z, y, (x + 1) % 4, zh, core), dev(z, y, (x + 3) % 4, zh, core)
    far_y, up_y, down_y = (y + 2) % 4, (y + 1) % 4, (y + 3) % 4
    far_x, up_x, down_x = (x + 2) % 4, (x + 1) % 4, (x + 3) % 4

    def back(t, zz, src):
        dst = lands.at[t, z % 2, core]
        return src, dst, l_send.at[t, zz], l_recv.at[t, z % 2, core], zz

    def start_back(src, dst, send_sem, recv_sem, zz):
        here = jnp.logical_and(z == zz, z // 2 == core)

        @pl.when(here)
        def _():
            pltpu.make_async_copy(src, dst, recv_sem).start()

        @pl.when(jnp.logical_not(here))
        def _():
            copy_to(src, dst, send_sem, recv_sem, dev(zz, y, x, zh, z // 2)).start()

    def sent_back(src, dst, send_sem, recv_sem, zz):
        here = jnp.logical_and(z == zz, z // 2 == core)

        @pl.when(jnp.logical_not(here))
        def _():
            copy_to(src, dst, send_sem, recv_sem, dev(zz, y, x, zh, z // 2)).wait_send()

    def landed(t):
        for j in (0, 1):
            for r in (0, 1):
                arrive(lands.at[t, j, r], l_recv.at[t, j, r], l_send.at[t, 0])

    def copy_out(t, out_ref):
        for j in (0, 1):
            for r in (0, 1):
                out_ref[r * 256 : (r + 1) * 256, j * 128 : (j + 1) * 128] = lands[t, j, r]

    for zz in range(4):
        start_back(*back(0, zz, o_ref.at[zz]))
    y_order = (far_y, up_y, down_y, y)
    for n, yy in enumerate(y_order):
        send(p_ref.at[yy, 1 - core], parts_in.at[n], ps_send.at[n], ps_recv.at[n], sibling)
    for zz in range(4):
        start_back(*back(1, zz, dq_ref.at[zz]))

    landed(0)
    copy_out(0, attn)

    def term(to_core, xx):
        for k in (0, 1):
            at = pl.multiple_of((xx * 4 + k * 2 + to_core) * 256, 256)
            terms[to_core, xx, k] = jnp.dot(
                attn[...], w_ref[:, pl.ds(at, 256)], preferred_element_type=F32
            ).astype(BF16)

    x_order = (far_x, up_x, down_x, x)
    for n, xx in enumerate(x_order):
        term(1 - core, xx)
        send(
            terms.at[1 - core, xx], terms_in.at[n], xs_send.at[n], xs_recv.at[n], sibling
        )

    def add_parts(n, yy):
        arrive(parts_in.at[n], ps_recv.at[n], ps_send.at[n])

        def step(i, carry):
            zz, t = i // 2, i % 2
            parts[yy, zz, t] = (
                p_ref[yy, core, zz, t].astype(F32) + parts_in[n, zz, t].astype(F32)
            ).astype(BF16)
            return carry

        lax.fori_loop(0, 8, step, 0)

    add_parts(0, far_y)
    send(parts.at[far_y, pl.ds(0, 2)], ya, y_send.at[0], y_recv.at[0], y_up)
    send(parts.at[far_y, pl.ds(2, 2)], yb, y_send.at[1], y_recv.at[1], y_down)

    def add_terms(n, xx):
        term(core, xx)
        arrive(terms_in.at[n], xs_recv.at[n], xs_send.at[n])
        for k in (0, 1):
            terms[core, xx, k] = (
                terms[core, xx, k].astype(F32) + terms_in[n, k].astype(F32)
            ).astype(BF16)

    add_terms(0, far_x)
    send(terms.at[core, far_x, 0], xa, x_send.at[0], x_recv.at[0], x_up)
    send(terms.at[core, far_x, 1], xb, x_send.at[1], x_recv.at[1], x_down)
    add_parts(1, up_y)
    add_parts(2, down_y)
    add_terms(1, up_x)
    add_terms(2, down_x)

    arrive(ya, y_recv.at[0], y_send.at[0])
    for zz in (0, 1):
        parts[up_y, zz] = (parts[up_y, zz].astype(F32) + ya[zz].astype(F32)).astype(BF16)
    send(parts.at[up_y], yc, y_send.at[2], y_recv.at[2], y_up)
    arrive(yb, y_recv.at[1], y_send.at[1])
    for zz in (0, 1):
        parts[down_y, zz + 2] = (
            parts[down_y, zz + 2].astype(F32) + yb[zz].astype(F32)
        ).astype(BF16)
    send(parts.at[down_y], yd, y_send.at[3], y_recv.at[3], y_down)

    arrive(xa, x_recv.at[0], x_send.at[0])
    terms[core, up_x, 0] = (terms[core, up_x, 0].astype(F32) + xa[...].astype(F32)).astype(BF16)
    send(terms.at[core, up_x], xc, x_send.at[2], x_recv.at[2], x_up)
    arrive(xb, x_recv.at[1], x_send.at[1])
    terms[core, down_x, 1] = (
        terms[core, down_x, 1].astype(F32) + xb[...].astype(F32)
    ).astype(BF16)
    send(terms.at[core, down_x], xd, x_send.at[3], x_recv.at[3], x_down)

    add_terms(3, x)
    arrive(parts_in.at[3], ps_recv.at[3], ps_send.at[3])
    landed(1)
    copy_out(1, dqo_ref)

    arrive(xc, x_recv.at[2], x_send.at[2])
    arrive(xd, x_recv.at[3], x_send.at[3])

    def add_total(k):
        total[k] = (
            terms[core, x, k].astype(F32) + xc[k].astype(F32) + xd[k].astype(F32)
        ).astype(BF16)

    add_total(1 - zh)
    send(total.at[1 - zh], zb, z_send.at[0], z_recv.at[0], dev(z, y, x, 1 - zh, core))
    add_total(zh)

    arrive(yc, y_recv.at[2], y_send.at[2])
    arrive(yd, y_recv.at[3], y_send.at[3])

    def add_final(i, carry):
        zz, t = i // 2, i % 2
        final[zz, t] = (
            p_ref[y, core, zz, t].astype(F32)
            + parts_in[3, zz, t].astype(F32)
            + yc[zz, t].astype(F32)
            + yd[zz, t].astype(F32)
        ).astype(BF16)
        return carry

    lax.fori_loop(0, 8, add_final, 0)
    for zz in range(4):
        for t in (0, 1):
            start_back(*back(2 + t, zz, final.at[zz, t]))

    arrive(zb, z_recv.at[0], z_send.at[0])
    mixed_ref[...] = (total[zh].astype(F32) + zb[...].astype(F32)).astype(BF16)
    landed(2)
    copy_out(2, dko_ref)
    landed(3)
    copy_out(3, dvo_ref)
    for zz in range(4):
        sent_back(*back(0, zz, o_ref.at[zz]))
        sent_back(*back(1, zz, dq_ref.at[zz]))
        for t in (0, 1):
            sent_back(*back(2 + t, zz, final.at[zz, t]))
    for copy in sent:
        copy.wait_send()


def scatter(o, dq, dkv, w):
    vmem = pl.BlockSpec(memory_space=pltpu.VMEM)
    dma = pltpu.SemaphoreType.DMA
    return pl.pallas_call(
        scatter_kernel,
        out_shape=(jax.ShapeDtypeStruct((512, 256), BF16),) * 4,
        in_specs=[vmem] * 4,
        out_specs=(vmem,) * 4,
        scratch_shapes=[
            pltpu.VMEM((4, 2, 2, 256, 128), BF16),
            pltpu.VMEM((512, 256), BF16),
            pltpu.VMEM((2, 4, 2, 512, 256), BF16),
            pltpu.VMEM((4, 2, 512, 256), BF16),
            pltpu.VMEM((512, 256), BF16),
            pltpu.VMEM((512, 256), BF16),
            pltpu.VMEM((2, 512, 256), BF16),
            pltpu.VMEM((2, 512, 256), BF16),
            pltpu.VMEM((2, 512, 256), BF16),
            pltpu.VMEM((512, 256), BF16),
            pltpu.VMEM((4, 4, 2, 256, 128), BF16),
            pltpu.VMEM((4, 4, 2, 256, 128), BF16),
            pltpu.VMEM((2, 2, 256, 128), BF16),
            pltpu.VMEM((2, 2, 256, 128), BF16),
            pltpu.VMEM((4, 2, 256, 128), BF16),
            pltpu.VMEM((4, 2, 256, 128), BF16),
            pltpu.VMEM((4, 2, 256, 128), BF16),
            dma((4, 4)),
            dma((4, 2, 2)),
            dma((4,)),
            dma((4,)),
            dma((4,)),
            dma((4,)),
            dma((4,)),
            dma((4,)),
            dma((4,)),
            dma((4,)),
            dma((1,)),
            dma((1,)),
        ],
        compiler_params=pltpu.CompilerParams(
            collective_id=1, has_side_effects=True, vmem_limit_bytes=VMEM_LIMIT
        ),
        name="scatter_heads",
    )(o, dq, dkv, w)


def body(queries, keys, values, w_out, d_mixed, random_blocks, global_blocks):
    rb = jnp.pad(random_blocks, ((0, 4), (0, 125)))
    kv, q, da, rb = gather(queries, keys, values, d_mixed, w_out, rb)
    o, dq, dkv = attention(
        rb,
        global_blocks,
        kv.reshape(128, BLOCK, HEAD_DIM),
        q.reshape(8, BLOCK, HEAD_DIM),
        da.reshape(8, BLOCK, HEAD_DIM),
    )
    return scatter(
        o.reshape(4, 256, 128),
        dq.reshape(4, 256, 128),
        dkv.reshape(4, 2, 4, 2, 256, 128),
        w_out,
    )


def solution(mesh):
    return jax.shard_map(
        body,
        mesh=mesh,
        in_specs=(
            P("seq", "head"),
            P("seq", "head"),
            P("seq", "head"),
            P("head", None),
            P("seq", "head"),
            P("seq", None),
            P(),
        ),
        out_specs=(P("seq", "head"), P("seq", "head"), P("seq", "head"), P("seq", "head")),
        check_vma=False,
    )
```

```python
import jax
import jax.numpy as jnp
from jax import lax
from jax.experimental import pallas as pl
from jax.experimental.pallas import tpu as pltpu
from jax.sharding import PartitionSpec as P

HEAD_DIM = 128
BLOCK = 128
SLOTS = 8
MASKED = -1e30
CONTRACT_LAST = (((1,), (1,)), ((), ()))
CONTRACT_FIRST = (((0,), (0,)), ((), ()))
MESH = pl.DeviceIdType.MESH
BF16 = jnp.bfloat16
F32 = jnp.float32
VMEM_LIMIT = 56 * 1024 * 1024


def place():
    seq, head = lax.axis_index("seq"), lax.axis_index("head")
    return seq // 4, seq % 4, head // 4, (head // 2) % 2, head % 2


def dev(z, y, x, zh, core):
    return (z * 4 + y, x * 4 + zh * 2 + core)


def copy_to(src, dst, send_sem, recv_sem, device):
    return pltpu.make_async_remote_copy(
        src_ref=src,
        dst_ref=dst,
        send_sem=send_sem,
        recv_sem=recv_sem,
        device_id=device,
        device_id_type=MESH,
    )


def greet():
    z, y, x, zh, core = place()
    barrier = pltpu.get_barrier_semaphore()
    others = [dev(z, y, x, zh, 1 - core)]
    for step in (1, 2, 3):
        for r in (0, 1):
            others.append(dev((z + step) % 4, y, x, zh, r))
    others += [dev(z, (y + 1) % 4, x, zh, core), dev(z, (y + 3) % 4, x, zh, core)]
    others += [dev(z, y, (x + 1) % 4, zh, core), dev(z, y, (x + 3) % 4, zh, core)]
    others.append(dev(z, y, x, 1 - zh, core))
    for other in others:
        pl.semaphore_signal(barrier, inc=1, device_id=other, device_id_type=MESH)
    pl.semaphore_wait(barrier, len(others))


def slot_table(random_ref, global_ref):
    first = lax.axis_index("seq") * 4
    rows = lax.broadcasted_iota(jnp.int32, (8, 128), 0)
    lanes = lax.broadcasted_iota(jnp.int32, (8, 128), 1)
    table = jnp.zeros((8, 128), jnp.int32)
    for i in range(4):
        own = first + i
        ids = [own - 1, own, own + 1]
        ids += [random_ref[i, t] for t in range(3)]
        ids += [global_ref[t] for t in range(2)]
        for t, block in enumerate(ids):
            dead = jnp.logical_or(block < 0, block > 63)
            for earlier in ids[:t]:
                dead = jnp.logical_or(dead, block == earlier)
            block = jnp.minimum(jnp.maximum(block, 0), 63)
            at = ((block >> 2) & 3) * 32 + ((block >> 1) & 1) * 16 + (block >> 4) * 2 + (block & 1)
            here = rows == i
            table = jnp.where(jnp.logical_and(here, lanes == t), at, table)
            table = jnp.where(
                jnp.logical_and(here, lanes == SLOTS + t), dead.astype(jnp.int32), table
            )
    return table


def gather_kernel(
    q_ref,
    k_ref,
    v_ref,
    dm_ref,
    w_ref,
    random_ref,
    global_ref,
    tables_ref,
    qm_ref,
    da_ref,
    probs_ref,
    scores_ref,
    dq_ref,
    ol_ref,
    kv_ref,
    table_ref,
    dm_all,
    grad,
    grad_acc,
    ids_ref,
    outs,
    full,
    kcat,
    vcat,
    id_sem,
    a_send,
    a_recv,
    b_send,
    b_recv,
    y_send,
    y_recv,
    ys_send,
    ys_recv,
    z_send,
    z_recv,
    x_send,
    x_recv,
    xs_send,
    xs_recv,
    g_send,
    g_recv,
    o_send,
    o_recv,
):
    z, y, x, zh, core = place()
    sibling = dev(z, y, x, zh, 1 - core)
    sent = []
    table_ref[...] = slot_table(random_ref, global_ref)
    greet()

    def send(src, dst, send_sem, recv_sem, device):
        copy = copy_to(src, dst, send_sem, recv_sem, device)
        copy.start()
        sent.append(copy)

    def arrive(dst, recv_sem, send_sem):
        copy_to(dst, dst, send_sem, recv_sem, sibling).wait_recv()

    y_up, y_down = dev(z, (y + 1) % 4, x, zh, core), dev(z, (y + 3) % 4, x, zh, core)
    x_up, x_down = dev(z, y, (x + 1) % 4, zh, core), dev(z, y, (x + 3) % 4, zh, core)
    partner = dev(z, y, x, 1 - zh, core)
    y_of = (y, (y + 3) % 4, (y + 1) % 4, (y + 2) % 4)
    x_of = (x, (x + 3) % 4, (x + 1) % 4, (x + 2) % 4)

    def to_line(src, dst, send_sem, recv_sem, j, r):
        there = 2 * core + j
        here = jnp.logical_and(there == z, core == r)

        @pl.when(here)
        def _():
            pltpu.make_async_copy(src, dst, recv_sem).start()

        @pl.when(jnp.logical_not(here))
        def _():
            copy_to(src, dst, send_sem, recv_sem, dev(there, y, x, zh, r)).start()

    def line_sent(src, dst, send_sem, recv_sem, j, r):
        there = 2 * core + j
        here = jnp.logical_and(there == z, core == r)

        @pl.when(jnp.logical_not(here))
        def _():
            copy_to(src, dst, send_sem, recv_sem, dev(there, y, x, zh, r)).wait_send()

    def piece(src, j, r):
        return src.at[pl.ds(2 * r, 2), :, pl.ds(j * 128, 128)]

    def kv_at(yy, r, t, zz, count):
        return kv_ref.at[pl.ds((((yy * 2 + r) * 2 + t) * 4 + zz) * 2, 2 * count)]

    def kv_args(t):
        for j in (0, 1):
            for r in (0, 1):
                yield (
                    piece((k_ref, v_ref)[t], j, r),
                    kv_at(y, r, t, z, 1),
                    a_send.at[t, j, r],
                    a_recv.at[t, z],
                    j,
                    r,
                )

    def query_args():
        for j in (0, 1):
            for r in (0, 1):
                yield (
                    piece(q_ref, j, r),
                    qm_ref.at[pl.ds(2 * z, 2)],
                    a_send.at[2, j, r],
                    a_recv.at[2, z],
                    j,
                    r,
                )

    def grad_args(r):
        for j in (0, 1):
            yield (
                piece(grad, j, r),
                da_ref.at[pl.ds(2 * z, 2)],
                g_send.at[j, r],
                g_recv.at[z],
                j,
                r,
            )

    def dm_block(wave, slot, late):
        return dm_all.at[wave, core, x_of[slot], (1 - zh) if late else zh]

    def own_rows(wave):
        return dm_ref.at[pl.ds(wave * 256, 256)]

    def dm_to_sibling(wave, slot, late, src):
        k = (1 - zh) if late else zh
        send(
            src,
            dm_block(wave, slot, late),
            xs_send.at[wave, slot, late],
            xs_recv.at[wave, x_of[slot], k],
            sibling,
        )

    def dm_to_ring(wave, late, src):
        dst = dm_block(wave, 0, late)
        send(src, dst, x_send.at[wave, late, 0], x_recv.at[wave, late, 0], x_up)
        send(src, dst, x_send.at[wave, late, 1], x_recv.at[wave, late, 1], x_down)
        dm_to_sibling(wave, 0, late, src)

    def dm_to_partner(wave):
        send(
            own_rows(wave),
            dm_block(wave, 0, 0),
            z_send.at[wave],
            z_recv.at[wave],
            partner,
        )

    def dm_from_partner(wave):
        block = dm_block(wave, 0, 1)
        arrive(block, z_recv.at[wave], z_send.at[wave])
        dm_to_ring(wave, 1, block)

    def dm_from_ring(wave, late):
        for side in (0, 1):
            block = dm_block(wave, 1 + side, late)
            arrive(block, x_recv.at[wave, late, side], x_send.at[wave, late, side])
            if side == (wave + late) % 2:
                send(
                    block,
                    block,
                    x_send.at[wave, late, 2],
                    x_recv.at[wave, late, 2],
                    (x_up, x_down)[side],
                )
            dm_to_sibling(wave, 1 + side, late, block)

    def dm_from_far(wave, late):
        block = dm_block(wave, 3, late)
        arrive(block, x_recv.at[wave, late, 2], x_send.at[wave, late, 2])
        dm_to_sibling(wave, 3, late, block)

    def kv_from_line(t):
        for zz in range(4):
            arrive(kv_at(y, core, t, zz, 1), a_recv.at[t, zz], a_send.at[t, 0, 0])
        own = kv_at(y, core, t, 0, 4)
        send(own, own, y_send.at[t, 0], y_recv.at[t, 0], y_up)
        send(own, own, y_send.at[t, 1], y_recv.at[t, 1], y_down)
        send(own, own, ys_send.at[t, 0], ys_recv.at[t, 0], sibling)

    def kv_from_ring(t):
        for side in (0, 1):
            block = kv_at(y_of[1 + side], core, t, 0, 4)
            arrive(block, y_recv.at[t, side], y_send.at[t, side])
            part = kv_at(y_of[1 + side], core, t, 2 * side, 2)
            send(
                part,
                part,
                y_send.at[t, 2 + side],
                y_recv.at[t, 2 + side],
                (y_up, y_down)[side],
            )
            send(block, block, ys_send.at[t, 1 + side], ys_recv.at[t, 1 + side], sibling)

    def kv_from_far(t):
        for side in (0, 1):
            part = kv_at(y_of[3], core, t, 2 * side, 2)
            arrive(part, y_recv.at[t, 2 + side], y_send.at[t, 2 + side])
        block = kv_at(y_of[3], core, t, 0, 4)
        send(block, block, ys_send.at[t, 3], ys_recv.at[t, 3], sibling)

    def add_product(wave, from_core, fresh):
        if fresh:
            grad_acc[...] = jnp.zeros_like(grad_acc)

        def step(i, carry):
            xx, k = i // 2, i % 2
            at = pl.multiple_of((xx * 4 + k * 2 + from_core) * 256, 256)
            grad_acc[...] += lax.dot_general(
                dm_all[wave, from_core, xx, k],
                w_ref[:, pl.ds(at, 256)],
                CONTRACT_LAST,
                preferred_element_type=F32,
            )
            return carry

        lax.fori_loop(0, 8, step, 0)

    def make_grad(wave):
        add_product(wave, core, True)
        for xx in range(4):
            for k in (0, 1):
                arrive(
                    dm_all.at[wave, 1 - core, xx, k],
                    xs_recv.at[wave, xx, k],
                    xs_send.at[wave, 0, 0],
                )
        add_product(wave, 1 - core, False)
        grad[2 * wave] = grad_acc[:128, :].astype(BF16)
        grad[2 * wave + 1] = grad_acc[128:, :].astype(BF16)
        for args in grad_args(wave):
            to_line(*args)

    for args in kv_args(0):
        to_line(*args)
    dm_to_partner(0)
    for wave in (0, 1):
        dm_to_ring(wave, 0, own_rows(wave))
    for args in kv_args(1):
        to_line(*args)
    dm_to_partner(1)
    for step in (1, 2, 3):
        send(
            table_ref,
            tables_ref.at[z],
            b_send.at[step - 1],
            b_recv.at[step - 1],
            dev((z + step) % 4, y, x, zh, core),
        )
    tables_ref[z] = table_ref[...]
    for wave in (0, 1):
        dm_all[wave, core, x, zh] = dm_ref[wave * 256 : (wave + 1) * 256, :]

    kv_from_line(0)
    dm_from_partner(0)
    dm_from_ring(0, 0)
    dm_from_ring(1, 0)
    kv_from_line(1)
    for args in query_args():
        to_line(*args)
    dm_from_partner(1)
    kv_from_ring(0)
    dm_from_ring(0, 1)
    kv_from_ring(1)
    dm_from_far(0, 0)
    dm_from_far(1, 0)
    dm_from_far(0, 1)
    dm_from_ring(1, 1)
    kv_from_far(0)
    make_grad(0)
    dm_from_far(1, 1)
    kv_from_far(1)
    make_grad(1)

    for step in (1, 2, 3):
        arrive(tables_ref.at[(z - step + 4) % 4], b_recv.at[step - 1], b_send.at[step - 1])
    to_smem = pltpu.make_async_copy(tables_ref, ids_ref, id_sem.at[0])
    to_smem.start()
    for t in (0, 1):
        for slot in range(4):
            arrive(kv_at(y_of[slot], 1 - core, t, 0, 4), ys_recv.at[t, slot], ys_send.at[t, 0])
    for zz in range(4):
        arrive(qm_ref.at[pl.ds(2 * zz, 2)], a_recv.at[2, zz], a_send.at[2, 0, 0])
    to_smem.wait()

    scale = HEAD_DIM ** (-0.5)

    def forward(n, carry):
        zz, i = n // 2, 2 * core + n % 2
        for t in range(SLOTS):
            at = ids_ref[zz, i, t]
            kcat[n, t * BLOCK : (t + 1) * BLOCK, :] = kv_ref[at]
            vcat[n, t * BLOCK : (t + 1) * BLOCK, :] = kv_ref[at + 8]
        bias = jnp.concatenate(
            [
                jnp.full((1, BLOCK), ids_ref[zz, i, SLOTS + t].astype(F32) * MASKED, F32)
                for t in range(SLOTS)
            ],
            axis=1,
        )
        scores = (
            lax.dot_general(qm_ref[n], kcat[n], CONTRACT_LAST, preferred_element_type=F32)
            * scale
            + bias
        )
        top = jnp.max(scores, axis=1, keepdims=True)
        powers = jnp.exp(scores - top)
        probs = powers * (1.0 / jnp.sum(powers, axis=1, keepdims=True))
        full[n] = probs
        half = probs.astype(BF16)
        probs_ref[n] = half
        outs[n] = jnp.dot(half, vcat[n], preferred_element_type=F32).astype(BF16)
        return carry

    lax.fori_loop(0, 8, forward, 0)

    def out_here(zz):
        return jnp.logical_and(z == zz, z // 2 == core)

    def out_piece(zz):
        return outs.at[pl.ds(2 * zz, 2)]

    def out_copy(zz):
        return copy_to(
            out_piece(zz),
            ol_ref.at[z % 2, core],
            o_send.at[zz],
            o_recv.at[z % 2, core],
            dev(zz, y, x, zh, z // 2),
        )

    for zz in range(4):

        @pl.when(out_here(zz))
        def _():
            pltpu.make_async_copy(
                out_piece(zz), ol_ref.at[z % 2, core], o_recv.at[z % 2, core]
            ).start()

        @pl.when(jnp.logical_not(out_here(zz)))
        def _():
            out_copy(zz).start()

    for zz in range(4):
        arrive(da_ref.at[pl.ds(2 * zz, 2)], g_recv.at[zz], g_send.at[0, 0])

    def backward(n, carry):
        grad_rows = da_ref[n]
        delta = jnp.sum(outs[n].astype(F32) * grad_rows.astype(F32), axis=1, keepdims=True)
        prob_grad = lax.dot_general(
            grad_rows, vcat[n], CONTRACT_LAST, preferred_element_type=F32
        )
        score_grad = (full[n] * (prob_grad - delta) * scale).astype(BF16)
        scores_ref[n] = score_grad
        dq_ref[n] = jnp.dot(score_grad, kcat[n], preferred_element_type=F32).astype(BF16)
        return carry

    lax.fori_loop(0, 8, backward, 0)

    for j in (0, 1):
        for r in (0, 1):
            arrive(ol_ref.at[j, r], o_recv.at[j, r], o_send.at[0])
    for t in (0, 1):
        for args in kv_args(t):
            line_sent(*args)
        for args in grad_args(t):
            line_sent(*args)
    for args in query_args():
        line_sent(*args)
    for zz in range(4):

        @pl.when(jnp.logical_not(out_here(zz)))
        def _():
            out_copy(zz).wait_send()

    for copy in sent:
        copy.wait_send()


def gather(q, k, v, dm, w, random_blocks, global_blocks):
    vmem = pl.BlockSpec(memory_space=pltpu.VMEM)
    smem = pl.BlockSpec(memory_space=pltpu.SMEM)
    dma = pltpu.SemaphoreType.DMA
    blocks = jax.ShapeDtypeStruct((8, BLOCK, HEAD_DIM), BF16)
    weights = jax.ShapeDtypeStruct((8, BLOCK, SLOTS * BLOCK), BF16)
    return pl.pallas_call(
        gather_kernel,
        out_shape=(
            jax.ShapeDtypeStruct((4, 8, 128), jnp.int32),
            blocks,
            blocks,
            weights,
            weights,
            blocks,
            jax.ShapeDtypeStruct((2, 2, 2, BLOCK, HEAD_DIM), BF16),
        ),
        in_specs=[vmem] * 5 + [smem] * 2,
        out_specs=(vmem,) * 7,
        scratch_shapes=[
            pltpu.VMEM((128, BLOCK, HEAD_DIM), BF16),
            pltpu.VMEM((8, 128), jnp.int32),
            pltpu.VMEM((2, 2, 4, 2, 256, 256), BF16),
            pltpu.VMEM((4, BLOCK, 256), BF16),
            pltpu.VMEM((256, 256), F32),
            pltpu.SMEM((4, 8, 128), jnp.int32),
            pltpu.VMEM((8, BLOCK, HEAD_DIM), BF16),
            pltpu.VMEM((8, BLOCK, SLOTS * BLOCK), F32),
            pltpu.VMEM((8, SLOTS * BLOCK, HEAD_DIM), BF16),
            pltpu.VMEM((8, SLOTS * BLOCK, HEAD_DIM), BF16),
            dma((1,)),
            dma((3, 2, 2)),
            dma((3, 4)),
            dma((3,)),
            dma((3,)),
            dma((2, 4)),
            dma((2, 4)),
            dma((2, 4)),
            dma((2, 4)),
            dma((2,)),
            dma((2,)),
            dma((2, 2, 3)),
            dma((2, 2, 3)),
            dma((2, 4, 2)),
            dma((2, 4, 2)),
            dma((2, 2)),
            dma((4,)),
            dma((4,)),
            dma((2, 2)),
        ],
        compiler_params=pltpu.CompilerParams(
            collective_id=0, has_side_effects=True, vmem_limit_bytes=VMEM_LIMIT
        ),
        name="gather_heads",
    )(q, k, v, dm, w, random_blocks, global_blocks)


def key_grads_kernel(ids_ref, q_ref, da_ref, probs_ref, scores_ref, dkv_ref, acc):
    core = place()[4]

    def clear(i, carry):
        acc[i] = jnp.zeros((BLOCK, HEAD_DIM), F32)
        return carry

    lax.fori_loop(0, 128, clear, 0, unroll=8)

    def one(n, carry):
        key_add = lax.dot_general(
            scores_ref[n], q_ref[n], CONTRACT_FIRST, preferred_element_type=F32
        )
        value_add = lax.dot_general(
            probs_ref[n], da_ref[n], CONTRACT_FIRST, preferred_element_type=F32
        )
        for t in range(SLOTS):
            at = ids_ref[n // 2, 2 * core + n % 2, t]
            acc[at] += key_add[t * BLOCK : (t + 1) * BLOCK, :]
            acc[at + 8] += value_add[t * BLOCK : (t + 1) * BLOCK, :]
        return carry

    lax.fori_loop(0, 8, one, 0, unroll=2)

    def finish(i, carry):
        dkv_ref[i] = acc[i].astype(BF16)
        return carry

    lax.fori_loop(0, 128, finish, 0, unroll=8)


def key_grads(ids, q, da, probs, scores):
    vmem = pl.BlockSpec(memory_space=pltpu.VMEM)
    smem = pl.BlockSpec(memory_space=pltpu.SMEM)
    return pl.pallas_call(
        key_grads_kernel,
        out_shape=jax.ShapeDtypeStruct((128, BLOCK, HEAD_DIM), BF16),
        in_specs=[smem, vmem, vmem, vmem, vmem],
        out_specs=vmem,
        scratch_shapes=[pltpu.VMEM((128, BLOCK, HEAD_DIM), F32)],
        compiler_params=pltpu.CompilerParams(vmem_limit_bytes=VMEM_LIMIT),
        name="key_grads",
    )(ids, q, da, probs, scores)


def unpack(pieces, out_ref):
    for j in (0, 1):
        for r in (0, 1):
            for low in (0, 1):
                row = (2 * r + low) * BLOCK
                out_ref[row : row + BLOCK, j * 128 : (j + 1) * 128] = pieces[j, r, low]


def scatter_kernel(
    ol_ref,
    dq_ref,
    p_ref,
    w_ref,
    mixed_ref,
    lands,
    attn,
    terms,
    terms_in,
    xa,
    xc,
    total,
    zb,
    parts,
    parts_in,
    ya,
    yc,
    final,
    l_send,
    l_recv,
    ps_send,
    ps_recv,
    y_send,
    y_recv,
    xs_send,
    xs_recv,
    x_send,
    x_recv,
    z_send,
    z_recv,
):
    z, y, x, zh, core = place()
    sibling = dev(z, y, x, zh, 1 - core)
    sent = []
    greet()

    def send(src, dst, send_sem, recv_sem, device):
        copy = copy_to(src, dst, send_sem, recv_sem, device)
        copy.start()
        sent.append(copy)

    def arrive(dst, recv_sem, send_sem):
        copy_to(dst, dst, send_sem, recv_sem, sibling).wait_recv()

    y_dev = (dev(z, (y + 1) % 4, x, zh, core), dev(z, (y + 3) % 4, x, zh, core))
    x_dev = (dev(z, y, (x + 1) % 4, zh, core), dev(z, y, (x + 3) % 4, zh, core))
    y_of = ((y + 2) % 4, (y + 1) % 4, (y + 3) % 4, y)
    x_of = ((x + 2) % 4, (x + 1) % 4, (x + 3) % 4, x)

    def back(t, zz, src):
        dst = lands.at[t, z % 2, core]
        return src, dst, l_send.at[t, zz], l_recv.at[t, z % 2, core], zz

    def start_back(src, dst, send_sem, recv_sem, zz):
        here = jnp.logical_and(z == zz, z // 2 == core)

        @pl.when(here)
        def _():
            pltpu.make_async_copy(src, dst, recv_sem).start()

        @pl.when(jnp.logical_not(here))
        def _():
            copy_to(src, dst, send_sem, recv_sem, dev(zz, y, x, zh, z // 2)).start()

    def sent_back(src, dst, send_sem, recv_sem, zz):
        here = jnp.logical_and(z == zz, z // 2 == core)

        @pl.when(jnp.logical_not(here))
        def _():
            copy_to(src, dst, send_sem, recv_sem, dev(zz, y, x, zh, z // 2)).wait_send()

    def landed(t):
        for j in (0, 1):
            for r in (0, 1):
                arrive(lands.at[t, j, r], l_recv.at[t, j, r], l_send.at[t, 0])

    def query_piece(zz):
        return dq_ref.at[pl.ds(2 * zz, 2)]

    def parts_to_sibling(t):
        for n in range(4):
            send(
                p_ref.at[y_of[n], 1 - core, t],
                parts_in.at[t, n],
                ps_send.at[t, n],
                ps_recv.at[t, n],
                sibling,
            )

    def add_parts(t, n, zz, more):
        value = p_ref[y_of[n], core, t, zz].astype(F32) + parts_in[t, n, zz].astype(F32)
        for ref in more:
            value += ref.astype(F32)
        return value.astype(BF16)

    def parts_here(t, n):
        arrive(parts_in.at[t, n], ps_recv.at[t, n], ps_send.at[t, n])

    def parts_far(t):
        parts_here(t, 0)
        for side in (0, 1):
            for zz in (2 * side, 2 * side + 1):
                parts[t, 0, zz] = add_parts(t, 0, zz, ())
            send(
                parts.at[t, 0, pl.ds(2 * side, 2)],
                ya.at[t, side],
                y_send.at[t, side],
                y_recv.at[t, side],
                y_dev[side],
            )

    def parts_near(t):
        for side in (0, 1):
            n = 1 + side
            parts_here(t, n)
            for zz in (2 - 2 * side, 3 - 2 * side):
                parts[t, n, zz] = add_parts(t, n, zz, ())
            arrive(ya.at[t, side], y_recv.at[t, side], y_send.at[t, side])
            for low in (0, 1):
                zz = 2 * side + low
                parts[t, n, zz] = add_parts(t, n, zz, (ya[t, side, low],))
            send(
                parts.at[t, n],
                yc.at[t, side],
                y_send.at[t, n + 1],
                y_recv.at[t, n + 1],
                y_dev[side],
            )

    def parts_end(t):
        parts_here(t, 3)
        for side in (0, 1):
            arrive(yc.at[t, side], y_recv.at[t, 2 + side], y_send.at[t, 2 + side])
        for zz in range(4):
            final[t, zz] = add_parts(t, 3, zz, (yc[t, 0, zz], yc[t, 1, zz]))
            start_back(*back(1 + t, zz, final.at[t, zz]))

    def make_terms(wave, to_core, n):
        for k in (0, 1):
            at = pl.multiple_of((x_of[n] * 4 + k * 2 + to_core) * 256, 256)
            terms[wave, to_core, n, k] = jnp.dot(
                attn[wave * 256 : (wave + 1) * 256, :],
                w_ref[:, pl.ds(at, 256)],
                preferred_element_type=F32,
            ).astype(BF16)

    def terms_to_sibling(wave):
        for n in range(4):
            make_terms(wave, 1 - core, n)
            send(
                terms.at[wave, 1 - core, n],
                terms_in.at[wave, n],
                xs_send.at[wave, n],
                xs_recv.at[wave, n],
                sibling,
            )

    def terms_here(wave, n):
        make_terms(wave, core, n)
        arrive(terms_in.at[wave, n], xs_recv.at[wave, n], xs_send.at[wave, n])

    def add_terms(wave, n, k, more):
        value = terms[wave, core, n, k].astype(F32) + terms_in[wave, n, k].astype(F32)
        for ref in more:
            value += ref.astype(F32)
        return value.astype(BF16)

    def terms_far(wave):
        terms_here(wave, 0)
        for k in (0, 1):
            terms[wave, core, 0, k] = add_terms(wave, 0, k, ())
            send(
                terms.at[wave, core, 0, k],
                xa.at[wave, k],
                x_send.at[wave, k],
                x_recv.at[wave, k],
                x_dev[k],
            )

    def terms_near(wave):
        for side in (0, 1):
            n = 1 + side
            terms_here(wave, n)
            arrive(xa.at[wave, side], x_recv.at[wave, side], x_send.at[wave, side])
            terms[wave, core, n, side] = add_terms(wave, n, side, (xa[wave, side],))
            terms[wave, core, n, 1 - side] = add_terms(wave, n, 1 - side, ())
            send(
                terms.at[wave, core, n],
                xc.at[wave, side],
                x_send.at[wave, n + 1],
                x_recv.at[wave, n + 1],
                x_dev[side],
            )

    def terms_end(wave):
        terms_here(wave, 3)
        for side in (0, 1):
            arrive(xc.at[wave, side], x_recv.at[wave, 2 + side], x_send.at[wave, 2 + side])

        def add_total(k):
            total[wave, k] = add_terms(wave, 3, k, (xc[wave, 0, k], xc[wave, 1, k]))

        add_total(1 - zh)
        send(
            total.at[wave, 1 - zh],
            zb.at[wave],
            z_send.at[wave],
            z_recv.at[wave],
            dev(z, y, x, 1 - zh, core),
        )
        add_total(zh)

    def mixed_end(wave):
        arrive(zb.at[wave], z_recv.at[wave], z_send.at[wave])
        mixed_ref[wave * 256 : (wave + 1) * 256, :] = (
            total[wave, zh].astype(F32) + zb[wave].astype(F32)
        ).astype(BF16)

    parts_to_sibling(0)
    parts_to_sibling(1)
    for zz in range(4):
        start_back(*back(0, zz, query_piece(zz)))
    unpack(ol_ref, attn)
    terms_to_sibling(0)
    parts_far(0)
    terms_to_sibling(1)
    terms_far(0)
    parts_far(1)
    terms_far(1)
    parts_near(0)
    terms_near(0)
    parts_near(1)
    terms_near(1)
    parts_end(0)
    terms_end(0)
    parts_end(1)
    terms_end(1)
    mixed_end(0)
    mixed_end(1)
    for t in range(3):
        landed(t)
    for zz in range(4):
        sent_back(*back(0, zz, query_piece(zz)))
        for t in (0, 1):
            sent_back(*back(1 + t, zz, final.at[t, zz]))
    for copy in sent:
        copy.wait_send()


def scatter(ol, dq, dkv, w):
    vmem = pl.BlockSpec(memory_space=pltpu.VMEM)
    dma = pltpu.SemaphoreType.DMA
    return pl.pallas_call(
        scatter_kernel,
        out_shape=(
            jax.ShapeDtypeStruct((512, 256), BF16),
            jax.ShapeDtypeStruct((3, 2, 2, 2, BLOCK, HEAD_DIM), BF16),
        ),
        in_specs=[vmem] * 4,
        out_specs=(vmem,) * 2,
        scratch_shapes=[
            pltpu.VMEM((512, 256), BF16),
            pltpu.VMEM((2, 2, 4, 2, 256, 256), BF16),
            pltpu.VMEM((2, 4, 2, 256, 256), BF16),
            pltpu.VMEM((2, 2, 256, 256), BF16),
            pltpu.VMEM((2, 2, 2, 256, 256), BF16),
            pltpu.VMEM((2, 2, 256, 256), BF16),
            pltpu.VMEM((2, 256, 256), BF16),
            pltpu.VMEM((2, 4, 4, 2, BLOCK, HEAD_DIM), BF16),
            pltpu.VMEM((2, 4, 4, 2, BLOCK, HEAD_DIM), BF16),
            pltpu.VMEM((2, 2, 2, 2, BLOCK, HEAD_DIM), BF16),
            pltpu.VMEM((2, 2, 4, 2, BLOCK, HEAD_DIM), BF16),
            pltpu.VMEM((2, 4, 2, BLOCK, HEAD_DIM), BF16),
            dma((3, 4)),
            dma((3, 2, 2)),
            dma((2, 4)),
            dma((2, 4)),
            dma((2, 4)),
            dma((2, 4)),
            dma((2, 4)),
            dma((2, 4)),
            dma((2, 4)),
            dma((2, 4)),
            dma((2,)),
            dma((2,)),
        ],
        compiler_params=pltpu.CompilerParams(
            collective_id=1, has_side_effects=True, vmem_limit_bytes=VMEM_LIMIT
        ),
        name="scatter_heads",
    )(ol, dq, dkv, w)


def unpack_kernel(mixed_ref, lands_ref, mixed_out, dq_out, dk_out, dv_out):
    mixed_out[...] = mixed_ref[...]
    unpack(lands_ref.at[0], dq_out)
    unpack(lands_ref.at[1], dk_out)
    unpack(lands_ref.at[2], dv_out)


def unpack_all(mixed, lands):
    vmem = pl.BlockSpec(memory_space=pltpu.VMEM)
    return pl.pallas_call(
        unpack_kernel,
        out_shape=(jax.ShapeDtypeStruct((512, 256), BF16),) * 4,
        in_specs=[vmem] * 2,
        out_specs=(vmem,) * 4,
        name="unpack_outputs",
    )(mixed, lands)


def body(queries, keys, values, w_out, d_mixed, random_blocks, global_blocks):
    by_block = (4, BLOCK, 2 * HEAD_DIM)
    ids, q, da, probs, scores, dq, ol = gather(
        queries.reshape(by_block),
        keys.reshape(by_block),
        values.reshape(by_block),
        d_mixed,
        w_out,
        random_blocks,
        global_blocks,
    )
    dkv = key_grads(ids, q, da, probs, scores)
    dkv = dkv.reshape(4, 2, 2, 4, 2, BLOCK, HEAD_DIM)
    return unpack_all(*scatter(ol, dq, dkv, w_out))


def solution(mesh):
    return jax.shard_map(
        body,
        mesh=mesh,
        in_specs=(
            P("seq", "head"),
            P("seq", "head"),
            P("seq", "head"),
            P("head", None),
            P("seq", "head"),
            P("seq", None),
            P(),
        ),
        out_specs=(P("seq", "head"), P("seq", "head"), P("seq", "head"), P("seq", "head")),
        check_vma=False,
    )
```

```python
import jax
import jax.numpy as jnp
from jax import lax
from jax.experimental import pallas as pl
from jax.experimental.pallas import tpu as pltpu
from jax.sharding import PartitionSpec as P

HEAD_DIM = 128
BLOCK = 128
SLOTS = 8
MASKED = -1e30
CONTRACT_LAST = (((1,), (1,)), ((), ()))
CONTRACT_FIRST = (((0,), (0,)), ((), ()))
MESH = pl.DeviceIdType.MESH
BF16 = jnp.bfloat16
F32 = jnp.float32
VMEM_LIMIT = 56 * 1024 * 1024


def place():
    seq, head = lax.axis_index("seq"), lax.axis_index("head")
    return seq // 4, seq % 4, head // 4, (head // 2) % 2, head % 2


def dev(z, y, x, zh, core):
    return (z * 4 + y, x * 4 + zh * 2 + core)


def copy_to(src, dst, send_sem, recv_sem, device):
    return pltpu.make_async_remote_copy(
        src_ref=src,
        dst_ref=dst,
        send_sem=send_sem,
        recv_sem=recv_sem,
        device_id=device,
        device_id_type=MESH,
    )


def greet():
    z, y, x, zh, core = place()
    barrier = pltpu.get_barrier_semaphore()
    others = [dev(z, y, x, zh, 1 - core)]
    for step in (1, 2, 3):
        for r in (0, 1):
            others.append(dev((z + step) % 4, y, x, zh, r))
    others += [dev(z, (y + 1) % 4, x, zh, core), dev(z, (y + 3) % 4, x, zh, core)]
    others += [dev(z, y, (x + 1) % 4, zh, core), dev(z, y, (x + 3) % 4, zh, core)]
    others.append(dev(z, y, x, 1 - zh, core))
    for other in others:
        pl.semaphore_signal(barrier, inc=1, device_id=other, device_id_type=MESH)
    pl.semaphore_wait(barrier, len(others))


def slot_table(random_ref, global_ref):
    first = lax.axis_index("seq") * 4
    rows = lax.broadcasted_iota(jnp.int32, (8, 128), 0)
    lanes = lax.broadcasted_iota(jnp.int32, (8, 128), 1)
    table = jnp.zeros((8, 128), jnp.int32)
    for i in range(4):
        own = first + i
        ids = [own - 1, own, own + 1]
        ids += [random_ref[i, t] for t in range(3)]
        ids += [global_ref[t] for t in range(2)]
        for t, block in enumerate(ids):
            dead = jnp.logical_or(block < 0, block > 63)
            for earlier in ids[:t]:
                dead = jnp.logical_or(dead, block == earlier)
            block = jnp.minimum(jnp.maximum(block, 0), 63)
            at = ((block >> 2) & 3) * 32 + ((block >> 1) & 1) * 16 + (block >> 4) * 2 + (block & 1)
            here = rows == i
            table = jnp.where(jnp.logical_and(here, lanes == t), at, table)
            table = jnp.where(
                jnp.logical_and(here, lanes == SLOTS + t), dead.astype(jnp.int32), table
            )
    return table


def gather_kernel(
    q_ref,
    k_ref,
    v_ref,
    dm_ref,
    w_hbm,
    random_ref,
    global_ref,
    tables_ref,
    qm_ref,
    da_ref,
    probs_hbm,
    scores_hbm,
    dq_ref,
    ol_ref,
    w_ref,
    probs_ref,
    scores_ref,
    kv_ref,
    table_ref,
    dm_all,
    grad,
    grad_acc,
    ids_ref,
    outs,
    full,
    kcat,
    vcat,
    id_sem,
    a_send,
    a_recv,
    b_send,
    b_recv,
    y_send,
    y_recv,
    ys_send,
    ys_recv,
    z_send,
    z_recv,
    x_send,
    x_recv,
    xs_send,
    xs_recv,
    g_send,
    g_recv,
    o_send,
    o_recv,
):
    z, y, x, zh, core = place()
    sibling = dev(z, y, x, zh, 1 - core)
    sent = []
    load_w = pltpu.make_async_copy(w_hbm, w_ref, id_sem.at[1])
    load_w.start()
    table_ref[...] = slot_table(random_ref, global_ref)
    greet()

    def send(src, dst, send_sem, recv_sem, device):
        copy = copy_to(src, dst, send_sem, recv_sem, device)
        copy.start()
        sent.append(copy)

    def arrive(dst, recv_sem, send_sem):
        copy_to(dst, dst, send_sem, recv_sem, sibling).wait_recv()

    y_up, y_down = dev(z, (y + 1) % 4, x, zh, core), dev(z, (y + 3) % 4, x, zh, core)
    x_up, x_down = dev(z, y, (x + 1) % 4, zh, core), dev(z, y, (x + 3) % 4, zh, core)
    partner = dev(z, y, x, 1 - zh, core)
    y_of = (y, (y + 3) % 4, (y + 1) % 4, (y + 2) % 4)
    x_of = (x, (x + 3) % 4, (x + 1) % 4, (x + 2) % 4)

    def to_line(src, dst, send_sem, recv_sem, j, r):
        there = 2 * core + j
        here = jnp.logical_and(there == z, core == r)

        @pl.when(here)
        def _():
            pltpu.make_async_copy(src, dst, recv_sem).start()

        @pl.when(jnp.logical_not(here))
        def _():
            copy_to(src, dst, send_sem, recv_sem, dev(there, y, x, zh, r)).start()

    def line_sent(src, dst, send_sem, recv_sem, j, r):
        there = 2 * core + j
        here = jnp.logical_and(there == z, core == r)

        @pl.when(jnp.logical_not(here))
        def _():
            copy_to(src, dst, send_sem, recv_sem, dev(there, y, x, zh, r)).wait_send()

    def piece(src, j, r):
        return src.at[pl.ds(2 * r, 2), :, pl.ds(j * 128, 128)]

    def kv_at(yy, r, t, zz, count):
        return kv_ref.at[pl.ds((((yy * 2 + r) * 2 + t) * 4 + zz) * 2, 2 * count)]

    def kv_args(t):
        for j in (0, 1):
            for r in (0, 1):
                yield (
                    piece((k_ref, v_ref)[t], j, r),
                    kv_at(y, r, t, z, 1),
                    a_send.at[t, j, r],
                    a_recv.at[t, z],
                    j,
                    r,
                )

    def query_args():
        for j in (0, 1):
            for r in (0, 1):
                yield (
                    piece(q_ref, j, r),
                    qm_ref.at[pl.ds(2 * z, 2)],
                    a_send.at[2, j, r],
                    a_recv.at[2, z],
                    j,
                    r,
                )

    def grad_args(r):
        for j in (0, 1):
            yield (
                piece(grad, j, r),
                da_ref.at[pl.ds(2 * z, 2)],
                g_send.at[j, r],
                g_recv.at[z],
                j,
                r,
            )

    def dm_block(wave, slot, late):
        return dm_all.at[wave, core, x_of[slot], (1 - zh) if late else zh]

    def own_rows(wave):
        return dm_ref.at[pl.ds(wave * 256, 256)]

    def dm_to_sibling(wave, slot, late, src):
        k = (1 - zh) if late else zh
        send(
            src,
            dm_block(wave, slot, late),
            xs_send.at[wave, slot, late],
            xs_recv.at[wave, x_of[slot], k],
            sibling,
        )

    def dm_to_ring(wave, late, src):
        dst = dm_block(wave, 0, late)
        send(src, dst, x_send.at[wave, late, 0], x_recv.at[wave, late, 0], x_up)
        send(src, dst, x_send.at[wave, late, 1], x_recv.at[wave, late, 1], x_down)
        dm_to_sibling(wave, 0, late, src)

    def dm_to_partner(wave):
        send(
            own_rows(wave),
            dm_block(wave, 0, 0),
            z_send.at[wave],
            z_recv.at[wave],
            partner,
        )

    def dm_from_partner(wave):
        block = dm_block(wave, 0, 1)
        arrive(block, z_recv.at[wave], z_send.at[wave])
        dm_to_ring(wave, 1, block)

    def dm_from_ring(wave, late):
        for side in (0, 1):
            block = dm_block(wave, 1 + side, late)
            arrive(block, x_recv.at[wave, late, side], x_send.at[wave, late, side])
            if side == (wave + late) % 2:
                send(
                    block,
                    block,
                    x_send.at[wave, late, 2],
                    x_recv.at[wave, late, 2],
                    (x_up, x_down)[side],
                )
            dm_to_sibling(wave, 1 + side, late, block)

    def dm_from_far(wave, late):
        block = dm_block(wave, 3, late)
        arrive(block, x_recv.at[wave, late, 2], x_send.at[wave, late, 2])
        dm_to_sibling(wave, 3, late, block)

    def kv_from_line(t):
        for zz in range(4):
            arrive(kv_at(y, core, t, zz, 1), a_recv.at[t, zz], a_send.at[t, 0, 0])
        own = kv_at(y, core, t, 0, 4)
        send(own, own, y_send.at[t, 0], y_recv.at[t, 0], y_up)
        send(own, own, y_send.at[t, 1], y_recv.at[t, 1], y_down)
        send(own, own, ys_send.at[t, 0], ys_recv.at[t, 0], sibling)

    def kv_from_ring(t):
        for side in (0, 1):
            block = kv_at(y_of[1 + side], core, t, 0, 4)
            arrive(block, y_recv.at[t, side], y_send.at[t, side])
            part = kv_at(y_of[1 + side], core, t, 2 * side, 2)
            send(
                part,
                part,
                y_send.at[t, 2 + side],
                y_recv.at[t, 2 + side],
                (y_up, y_down)[side],
            )
            send(block, block, ys_send.at[t, 1 + side], ys_recv.at[t, 1 + side], sibling)

    def kv_from_far(t):
        for side in (0, 1):
            part = kv_at(y_of[3], core, t, 2 * side, 2)
            arrive(part, y_recv.at[t, 2 + side], y_send.at[t, 2 + side])
        block = kv_at(y_of[3], core, t, 0, 4)
        send(block, block, ys_send.at[t, 3], ys_recv.at[t, 3], sibling)

    def add_product(wave, from_core, fresh):
        if fresh:
            grad_acc[...] = jnp.zeros_like(grad_acc)

        def step(i, carry):
            xx, k = i // 2, i % 2
            at = pl.multiple_of((xx * 4 + k * 2 + from_core) * 256, 256)
            grad_acc[...] += lax.dot_general(
                dm_all[wave, from_core, xx, k],
                w_ref[:, pl.ds(at, 256)],
                CONTRACT_LAST,
                preferred_element_type=F32,
            )
            return carry

        lax.fori_loop(0, 8, step, 0)

    def make_grad(wave):
        add_product(wave, core, True)
        for xx in range(4):
            for k in (0, 1):
                arrive(
                    dm_all.at[wave, 1 - core, xx, k],
                    xs_recv.at[wave, xx, k],
                    xs_send.at[wave, 0, 0],
                )
        add_product(wave, 1 - core, False)
        grad[2 * wave] = grad_acc[:128, :].astype(BF16)
        grad[2 * wave + 1] = grad_acc[128:, :].astype(BF16)
        for args in grad_args(wave):
            to_line(*args)

    for args in kv_args(0):
        to_line(*args)
    dm_to_partner(0)
    for wave in (0, 1):
        dm_to_ring(wave, 0, own_rows(wave))
    for args in kv_args(1):
        to_line(*args)
    dm_to_partner(1)
    for step in (1, 2, 3):
        send(
            table_ref,
            tables_ref.at[z],
            b_send.at[step - 1],
            b_recv.at[step - 1],
            dev((z + step) % 4, y, x, zh, core),
        )
    tables_ref[z] = table_ref[...]
    for wave in (0, 1):
        dm_all[wave, core, x, zh] = dm_ref[wave * 256 : (wave + 1) * 256, :]

    kv_from_line(0)
    dm_from_partner(0)
    dm_from_ring(0, 0)
    dm_from_ring(1, 0)
    kv_from_line(1)
    for args in query_args():
        to_line(*args)
    dm_from_partner(1)
    kv_from_ring(0)
    dm_from_ring(0, 1)
    kv_from_ring(1)
    dm_from_far(0, 0)
    dm_from_far(1, 0)
    dm_from_far(0, 1)
    dm_from_ring(1, 1)
    kv_from_far(0)
    load_w.wait()
    make_grad(0)
    dm_from_far(1, 1)
    kv_from_far(1)
    make_grad(1)

    for step in (1, 2, 3):
        arrive(tables_ref.at[(z - step + 4) % 4], b_recv.at[step - 1], b_send.at[step - 1])
    to_smem = pltpu.make_async_copy(tables_ref, ids_ref, id_sem.at[0])
    to_smem.start()
    for t in (0, 1):
        for slot in range(4):
            arrive(kv_at(y_of[slot], 1 - core, t, 0, 4), ys_recv.at[t, slot], ys_send.at[t, 0])
    for zz in range(4):
        arrive(qm_ref.at[pl.ds(2 * zz, 2)], a_recv.at[2, zz], a_send.at[2, 0, 0])
    to_smem.wait()

    scale = HEAD_DIM ** (-0.5)

    def forward(n, carry):
        zz, i = n // 2, 2 * core + n % 2
        for t in range(SLOTS):
            at = ids_ref[zz, i, t]
            kcat[n, t * BLOCK : (t + 1) * BLOCK, :] = kv_ref[at]
            vcat[n, t * BLOCK : (t + 1) * BLOCK, :] = kv_ref[at + 8]
        bias = jnp.concatenate(
            [
                jnp.full((1, BLOCK), ids_ref[zz, i, SLOTS + t].astype(F32) * MASKED, F32)
                for t in range(SLOTS)
            ],
            axis=1,
        )
        scores = (
            lax.dot_general(qm_ref[n], kcat[n], CONTRACT_LAST, preferred_element_type=F32)
            * scale
            + bias
        )
        top = jnp.max(scores, axis=1, keepdims=True)
        powers = jnp.exp(scores - top)
        probs = powers * (1.0 / jnp.sum(powers, axis=1, keepdims=True))
        full[n] = probs
        half = probs.astype(BF16)
        probs_ref[n] = half
        outs[n] = jnp.dot(half, vcat[n], preferred_element_type=F32).astype(BF16)
        return carry

    lax.fori_loop(0, 8, forward, 0, unroll=2)
    keep_probs = pltpu.make_async_copy(probs_ref, probs_hbm, id_sem.at[2])
    keep_probs.start()

    def out_here(zz):
        return jnp.logical_and(z == zz, z // 2 == core)

    def out_piece(zz):
        return outs.at[pl.ds(2 * zz, 2)]

    def out_copy(zz):
        return copy_to(
            out_piece(zz),
            ol_ref.at[z % 2, core],
            o_send.at[zz],
            o_recv.at[z % 2, core],
            dev(zz, y, x, zh, z // 2),
        )

    for zz in range(4):

        @pl.when(out_here(zz))
        def _():
            pltpu.make_async_copy(
                out_piece(zz), ol_ref.at[z % 2, core], o_recv.at[z % 2, core]
            ).start()

        @pl.when(jnp.logical_not(out_here(zz)))
        def _():
            out_copy(zz).start()

    for zz in range(4):
        arrive(da_ref.at[pl.ds(2 * zz, 2)], g_recv.at[zz], g_send.at[0, 0])

    def backward(n, carry):
        grad_rows = da_ref[n]
        delta = jnp.sum(outs[n].astype(F32) * grad_rows.astype(F32), axis=1, keepdims=True)
        prob_grad = lax.dot_general(
            grad_rows, vcat[n], CONTRACT_LAST, preferred_element_type=F32
        )
        score_grad = (full[n] * (prob_grad - delta) * scale).astype(BF16)
        scores_ref[n] = score_grad
        dq_ref[n] = jnp.dot(score_grad, kcat[n], preferred_element_type=F32).astype(BF16)
        return carry

    lax.fori_loop(0, 8, backward, 0, unroll=2)
    keep_scores = pltpu.make_async_copy(scores_ref, scores_hbm, id_sem.at[3])
    keep_scores.start()

    for j in (0, 1):
        for r in (0, 1):
            arrive(ol_ref.at[j, r], o_recv.at[j, r], o_send.at[0])
    for t in (0, 1):
        for args in kv_args(t):
            line_sent(*args)
        for args in grad_args(t):
            line_sent(*args)
    for args in query_args():
        line_sent(*args)
    for zz in range(4):

        @pl.when(jnp.logical_not(out_here(zz)))
        def _():
            out_copy(zz).wait_send()

    for copy in sent:
        copy.wait_send()
    keep_probs.wait()
    keep_scores.wait()


def gather(q, k, v, dm, w, random_blocks, global_blocks):
    vmem = pl.BlockSpec(memory_space=pltpu.VMEM)
    smem = pl.BlockSpec(memory_space=pltpu.SMEM)
    hbm = pl.BlockSpec(memory_space=pl.ANY)
    dma = pltpu.SemaphoreType.DMA
    blocks = jax.ShapeDtypeStruct((8, BLOCK, HEAD_DIM), BF16)
    weights = jax.ShapeDtypeStruct((8, BLOCK, SLOTS * BLOCK), BF16)
    return pl.pallas_call(
        gather_kernel,
        out_shape=(
            jax.ShapeDtypeStruct((4, 8, 128), jnp.int32),
            blocks,
            blocks,
            weights,
            weights,
            blocks,
            jax.ShapeDtypeStruct((2, 2, 2, BLOCK, HEAD_DIM), BF16),
        ),
        in_specs=[vmem] * 4 + [hbm] + [smem] * 2,
        out_specs=(vmem, vmem, vmem, hbm, hbm, vmem, vmem),
        scratch_shapes=[
            pltpu.VMEM((256, 4096), BF16),
            pltpu.VMEM((8, BLOCK, SLOTS * BLOCK), BF16),
            pltpu.VMEM((8, BLOCK, SLOTS * BLOCK), BF16),
            pltpu.VMEM((128, BLOCK, HEAD_DIM), BF16),
            pltpu.VMEM((8, 128), jnp.int32),
            pltpu.VMEM((2, 2, 4, 2, 256, 256), BF16),
            pltpu.VMEM((4, BLOCK, 256), BF16),
            pltpu.VMEM((256, 256), F32),
            pltpu.SMEM((4, 8, 128), jnp.int32),
            pltpu.VMEM((8, BLOCK, HEAD_DIM), BF16),
            pltpu.VMEM((8, BLOCK, SLOTS * BLOCK), F32),
            pltpu.VMEM((8, SLOTS * BLOCK, HEAD_DIM), BF16),
            pltpu.VMEM((8, SLOTS * BLOCK, HEAD_DIM), BF16),
            dma((4,)),
            dma((3, 2, 2)),
            dma((3, 4)),
            dma((3,)),
            dma((3,)),
            dma((2, 4)),
            dma((2, 4)),
            dma((2, 4)),
            dma((2, 4)),
            dma((2,)),
            dma((2,)),
            dma((2, 2, 3)),
            dma((2, 2, 3)),
            dma((2, 4, 2)),
            dma((2, 4, 2)),
            dma((2, 2)),
            dma((4,)),
            dma((4,)),
            dma((2, 2)),
        ],
        compiler_params=pltpu.CompilerParams(
            collective_id=0, has_side_effects=True, vmem_limit_bytes=VMEM_LIMIT
        ),
        name="gather_heads",
    )(q, k, v, dm, w, random_blocks, global_blocks)


def key_grads_kernel(
    ids_ref, q_ref, da_ref, probs_hbm, scores_hbm, dkv_hbm, acc, probs_ref, scores_ref, half, sems, out_sems
):
    core = place()[4]

    def load(part):
        rows = pl.ds(4 * part, 4)
        return (
            pltpu.make_async_copy(
                scores_hbm.at[rows], scores_ref.at[rows], sems.at[part, 0]
            ),
            pltpu.make_async_copy(probs_hbm.at[rows], probs_ref.at[rows], sems.at[part, 1]),
        )

    for part in (0, 1):
        for copy in load(part):
            copy.start()

    def clear(i, carry):
        acc[i] = jnp.zeros((BLOCK, HEAD_DIM), F32)
        return carry

    lax.fori_loop(0, 128, clear, 0, unroll=8)

    def one(n, carry):
        key_add = lax.dot_general(
            scores_ref[n], q_ref[n], CONTRACT_FIRST, preferred_element_type=F32
        )
        value_add = lax.dot_general(
            probs_ref[n], da_ref[n], CONTRACT_FIRST, preferred_element_type=F32
        )
        for t in range(SLOTS):
            at = ids_ref[n // 2, 2 * core + n % 2, t]
            acc[at] += key_add[t * BLOCK : (t + 1) * BLOCK, :]
            acc[at + 8] += value_add[t * BLOCK : (t + 1) * BLOCK, :]
        return carry

    for part in (0, 1):
        for copy in load(part):
            copy.wait()
        lax.fori_loop(4 * part, 4 * part + 4, one, 0, unroll=2)

    def store(part):
        rows = pl.ds(16 * part, 16)
        return pltpu.make_async_copy(half.at[rows], dkv_hbm.at[rows], out_sems.at[part])

    for part in range(8):

        def finish(i, carry):
            half[i] = acc[i].astype(BF16)
            return carry

        lax.fori_loop(16 * part, 16 * part + 16, finish, 0, unroll=8)
        store(part).start()
    for part in range(8):
        store(part).wait()


def key_grads(ids, q, da, probs, scores):
    vmem = pl.BlockSpec(memory_space=pltpu.VMEM)
    smem = pl.BlockSpec(memory_space=pltpu.SMEM)
    hbm = pl.BlockSpec(memory_space=pl.ANY)
    dma = pltpu.SemaphoreType.DMA
    return pl.pallas_call(
        key_grads_kernel,
        out_shape=jax.ShapeDtypeStruct((128, BLOCK, HEAD_DIM), BF16),
        in_specs=[smem, vmem, vmem, hbm, hbm],
        out_specs=hbm,
        scratch_shapes=[
            pltpu.VMEM((128, BLOCK, HEAD_DIM), F32),
            pltpu.VMEM((8, BLOCK, SLOTS * BLOCK), BF16),
            pltpu.VMEM((8, BLOCK, SLOTS * BLOCK), BF16),
            pltpu.VMEM((128, BLOCK, HEAD_DIM), BF16),
            dma((2, 2)),
            dma((8,)),
        ],
        compiler_params=pltpu.CompilerParams(vmem_limit_bytes=VMEM_LIMIT),
        name="key_grads",
    )(ids, q, da, probs, scores)


def unpack(pieces, out_ref):
    for j in (0, 1):
        for r in (0, 1):
            for low in (0, 1):
                row = (2 * r + low) * BLOCK
                out_ref[row : row + BLOCK, j * 128 : (j + 1) * 128] = pieces[j, r, low]


def scatter_kernel(
    ol_ref,
    dq_ref,
    p_hbm,
    w_hbm,
    mixed_ref,
    lands,
    w_ref,
    p_ref,
    load_sems,
    attn,
    terms,
    terms_in,
    xa,
    xc,
    total,
    zb,
    parts,
    parts_in,
    ya,
    yc,
    final,
    l_send,
    l_recv,
    ps_send,
    ps_recv,
    y_send,
    y_recv,
    xs_send,
    xs_recv,
    x_send,
    x_recv,
    z_send,
    z_recv,
):
    z, y, x, zh, core = place()
    sibling = dev(z, y, x, zh, 1 - core)
    sent = []
    load_w = pltpu.make_async_copy(w_hbm, w_ref, load_sems.at[0])
    load_p = pltpu.make_async_copy(p_hbm.at[:, core], p_ref, load_sems.at[1])
    load_w.start()
    load_p.start()
    unpack(ol_ref, attn)
    greet()

    def send(src, dst, send_sem, recv_sem, device):
        copy = copy_to(src, dst, send_sem, recv_sem, device)
        copy.start()
        sent.append(copy)

    def arrive(dst, recv_sem, send_sem):
        copy_to(dst, dst, send_sem, recv_sem, sibling).wait_recv()

    y_dev = (dev(z, (y + 1) % 4, x, zh, core), dev(z, (y + 3) % 4, x, zh, core))
    x_dev = (dev(z, y, (x + 1) % 4, zh, core), dev(z, y, (x + 3) % 4, zh, core))
    y_of = ((y + 2) % 4, (y + 1) % 4, (y + 3) % 4, y)
    x_of = ((x + 2) % 4, (x + 1) % 4, (x + 3) % 4, x)

    def back(t, zz, src):
        dst = lands.at[t, z % 2, core]
        return src, dst, l_send.at[t, zz], l_recv.at[t, z % 2, core], zz

    def start_back(src, dst, send_sem, recv_sem, zz):
        here = jnp.logical_and(z == zz, z // 2 == core)

        @pl.when(here)
        def _():
            pltpu.make_async_copy(src, dst, recv_sem).start()

        @pl.when(jnp.logical_not(here))
        def _():
            copy_to(src, dst, send_sem, recv_sem, dev(zz, y, x, zh, z // 2)).start()

    def sent_back(src, dst, send_sem, recv_sem, zz):
        here = jnp.logical_and(z == zz, z // 2 == core)

        @pl.when(jnp.logical_not(here))
        def _():
            copy_to(src, dst, send_sem, recv_sem, dev(zz, y, x, zh, z // 2)).wait_send()

    def landed(t):
        for j in (0, 1):
            for r in (0, 1):
                arrive(lands.at[t, j, r], l_recv.at[t, j, r], l_send.at[t, 0])

    def query_piece(zz):
        return dq_ref.at[pl.ds(2 * zz, 2)]

    def parts_to_sibling(t):
        for n in range(4):
            send(
                p_hbm.at[y_of[n], 1 - core, t],
                parts_in.at[t, n],
                ps_send.at[t, n],
                ps_recv.at[t, n],
                sibling,
            )

    def add_parts(t, n, zz, more):
        value = p_ref[y_of[n], t, zz].astype(F32) + parts_in[t, n, zz].astype(F32)
        for ref in more:
            value += ref.astype(F32)
        return value.astype(BF16)

    def parts_here(t, n):
        arrive(parts_in.at[t, n], ps_recv.at[t, n], ps_send.at[t, n])

    def parts_far(t):
        parts_here(t, 0)
        for side in (0, 1):
            for zz in (2 * side, 2 * side + 1):
                parts[t, 0, zz] = add_parts(t, 0, zz, ())
            send(
                parts.at[t, 0, pl.ds(2 * side, 2)],
                ya.at[t, side],
                y_send.at[t, side],
                y_recv.at[t, side],
                y_dev[side],
            )

    def parts_near(t):
        for side in (0, 1):
            n = 1 + side
            parts_here(t, n)
            for zz in (2 - 2 * side, 3 - 2 * side):
                parts[t, n, zz] = add_parts(t, n, zz, ())
            arrive(ya.at[t, side], y_recv.at[t, side], y_send.at[t, side])
            for low in (0, 1):
                zz = 2 * side + low
                parts[t, n, zz] = add_parts(t, n, zz, (ya[t, side, low],))
            send(
                parts.at[t, n],
                yc.at[t, side],
                y_send.at[t, n + 1],
                y_recv.at[t, n + 1],
                y_dev[side],
            )

    def parts_end(t):
        parts_here(t, 3)
        for side in (0, 1):
            arrive(yc.at[t, side], y_recv.at[t, 2 + side], y_send.at[t, 2 + side])
        for zz in range(4):
            final[t, zz] = add_parts(t, 3, zz, (yc[t, 0, zz], yc[t, 1, zz]))
            start_back(*back(1 + t, zz, final.at[t, zz]))

    def make_terms(wave, to_core, n):
        for k in (0, 1):
            at = pl.multiple_of((x_of[n] * 4 + k * 2 + to_core) * 256, 256)
            terms[wave, to_core, n, k] = jnp.dot(
                attn[wave * 256 : (wave + 1) * 256, :],
                w_ref[:, pl.ds(at, 256)],
                preferred_element_type=F32,
            ).astype(BF16)

    def terms_to_sibling(wave):
        for n in range(4):
            make_terms(wave, 1 - core, n)
            send(
                terms.at[wave, 1 - core, n],
                terms_in.at[wave, n],
                xs_send.at[wave, n],
                xs_recv.at[wave, n],
                sibling,
            )

    def terms_here(wave, n):
        make_terms(wave, core, n)
        arrive(terms_in.at[wave, n], xs_recv.at[wave, n], xs_send.at[wave, n])

    def add_terms(wave, n, k, more):
        value = terms[wave, core, n, k].astype(F32) + terms_in[wave, n, k].astype(F32)
        for ref in more:
            value += ref.astype(F32)
        return value.astype(BF16)

    def terms_far(wave):
        terms_here(wave, 0)
        for k in (0, 1):
            terms[wave, core, 0, k] = add_terms(wave, 0, k, ())
            send(
                terms.at[wave, core, 0, k],
                xa.at[wave, k],
                x_send.at[wave, k],
                x_recv.at[wave, k],
                x_dev[k],
            )

    def terms_near(wave):
        for side in (0, 1):
            n = 1 + side
            terms_here(wave, n)
            arrive(xa.at[wave, side], x_recv.at[wave, side], x_send.at[wave, side])
            terms[wave, core, n, side] = add_terms(wave, n, side, (xa[wave, side],))
            terms[wave, core, n, 1 - side] = add_terms(wave, n, 1 - side, ())
            send(
                terms.at[wave, core, n],
                xc.at[wave, side],
                x_send.at[wave, n + 1],
                x_recv.at[wave, n + 1],
                x_dev[side],
            )

    def terms_end(wave):
        terms_here(wave, 3)
        for side in (0, 1):
            arrive(xc.at[wave, side], x_recv.at[wave, 2 + side], x_send.at[wave, 2 + side])

        def add_total(k):
            total[wave, k] = add_terms(wave, 3, k, (xc[wave, 0, k], xc[wave, 1, k]))

        add_total(1 - zh)
        send(
            total.at[wave, 1 - zh],
            zb.at[wave],
            z_send.at[wave],
            z_recv.at[wave],
            dev(z, y, x, 1 - zh, core),
        )
        add_total(zh)

    def mixed_end(wave):
        arrive(zb.at[wave], z_recv.at[wave], z_send.at[wave])
        mixed_ref[wave * 256 : (wave + 1) * 256, :] = (
            total[wave, zh].astype(F32) + zb[wave].astype(F32)
        ).astype(BF16)

    parts_to_sibling(0)
    parts_to_sibling(1)
    for zz in range(4):
        start_back(*back(0, zz, query_piece(zz)))
    load_w.wait()
    terms_to_sibling(0)
    load_p.wait()
    parts_far(0)
    terms_to_sibling(1)
    terms_far(0)
    parts_far(1)
    terms_far(1)
    parts_near(0)
    terms_near(0)
    parts_near(1)
    terms_near(1)
    parts_end(0)
    terms_end(0)
    parts_end(1)
    terms_end(1)
    mixed_end(0)
    mixed_end(1)
    for t in range(3):
        landed(t)
    for zz in range(4):
        sent_back(*back(0, zz, query_piece(zz)))
        for t in (0, 1):
            sent_back(*back(1 + t, zz, final.at[t, zz]))
    for copy in sent:
        copy.wait_send()


def scatter(ol, dq, dkv, w):
    vmem = pl.BlockSpec(memory_space=pltpu.VMEM)
    hbm = pl.BlockSpec(memory_space=pl.ANY)
    dma = pltpu.SemaphoreType.DMA
    return pl.pallas_call(
        scatter_kernel,
        out_shape=(
            jax.ShapeDtypeStruct((512, 256), BF16),
            jax.ShapeDtypeStruct((3, 2, 2, 2, BLOCK, HEAD_DIM), BF16),
        ),
        in_specs=[vmem, vmem, hbm, hbm],
        out_specs=(vmem,) * 2,
        scratch_shapes=[
            pltpu.VMEM((256, 4096), BF16),
            pltpu.VMEM((4, 2, 4, 2, BLOCK, HEAD_DIM), BF16),
            dma((2,)),
            pltpu.VMEM((512, 256), BF16),
            pltpu.VMEM((2, 2, 4, 2, 256, 256), BF16),
            pltpu.VMEM((2, 4, 2, 256, 256), BF16),
            pltpu.VMEM((2, 2, 256, 256), BF16),
            pltpu.VMEM((2, 2, 2, 256, 256), BF16),
            pltpu.VMEM((2, 2, 256, 256), BF16),
            pltpu.VMEM((2, 256, 256), BF16),
            pltpu.VMEM((2, 4, 4, 2, BLOCK, HEAD_DIM), BF16),
            pltpu.VMEM((2, 4, 4, 2, BLOCK, HEAD_DIM), BF16),
            pltpu.VMEM((2, 2, 2, 2, BLOCK, HEAD_DIM), BF16),
            pltpu.VMEM((2, 2, 4, 2, BLOCK, HEAD_DIM), BF16),
            pltpu.VMEM((2, 4, 2, BLOCK, HEAD_DIM), BF16),
            dma((3, 4)),
            dma((3, 2, 2)),
            dma((2, 4)),
            dma((2, 4)),
            dma((2, 4)),
            dma((2, 4)),
            dma((2, 4)),
            dma((2, 4)),
            dma((2, 4)),
            dma((2, 4)),
            dma((2,)),
            dma((2,)),
        ],
        compiler_params=pltpu.CompilerParams(
            collective_id=1, has_side_effects=True, vmem_limit_bytes=VMEM_LIMIT
        ),
        name="scatter_heads",
    )(ol, dq, dkv, w)


def unpack_kernel(mixed_ref, lands_ref, mixed_out, dq_out, dk_out, dv_out):
    mixed_out[...] = mixed_ref[...]
    unpack(lands_ref.at[0], dq_out)
    unpack(lands_ref.at[1], dk_out)
    unpack(lands_ref.at[2], dv_out)


def unpack_all(mixed, lands):
    vmem = pl.BlockSpec(memory_space=pltpu.VMEM)
    return pl.pallas_call(
        unpack_kernel,
        out_shape=(jax.ShapeDtypeStruct((512, 256), BF16),) * 4,
        in_specs=[vmem] * 2,
        out_specs=(vmem,) * 4,
        name="unpack_outputs",
    )(mixed, lands)


def body(queries, keys, values, w_out, d_mixed, random_blocks, global_blocks):
    by_block = (4, BLOCK, 2 * HEAD_DIM)
    ids, q, da, probs, scores, dq, ol = gather(
        queries.reshape(by_block),
        keys.reshape(by_block),
        values.reshape(by_block),
        d_mixed,
        w_out,
        random_blocks,
        global_blocks,
    )
    dkv = key_grads(ids, q, da, probs, scores)
    dkv = dkv.reshape(4, 2, 2, 4, 2, BLOCK, HEAD_DIM)
    return unpack_all(*scatter(ol, dq, dkv, w_out))


def solution(mesh):
    return jax.shard_map(
        body,
        mesh=mesh,
        in_specs=(
            P("seq", "head"),
            P("seq", "head"),
            P("seq", "head"),
            P("head", None),
            P("seq", "head"),
            P("seq", None),
            P(),
        ),
        out_specs=(P("seq", "head"), P("seq", "head"), P("seq", "head"), P("seq", "head")),
        check_vma=False,
    )
```

```python
import jax
import jax.numpy as jnp
from jax import lax
from jax.experimental import pallas as pl
from jax.experimental.pallas import tpu as pltpu
from jax.sharding import PartitionSpec as P

HEAD_DIM = 128
BLOCK = 128
SLOTS = 8
MASKED = -1e30
CONTRACT_LAST = (((1,), (1,)), ((), ()))
CONTRACT_FIRST = (((0,), (0,)), ((), ()))
MESH = pl.DeviceIdType.MESH
BF16 = jnp.bfloat16
F32 = jnp.float32
VMEM_LIMIT = 56 * 1024 * 1024


def place():
    seq, head = lax.axis_index("seq"), lax.axis_index("head")
    return seq // 4, seq % 4, head // 4, (head // 2) % 2, head % 2


def dev(z, y, x, zh, core):
    return (z * 4 + y, x * 4 + zh * 2 + core)


def copy_to(src, dst, send_sem, recv_sem, device):
    return pltpu.make_async_remote_copy(
        src_ref=src,
        dst_ref=dst,
        send_sem=send_sem,
        recv_sem=recv_sem,
        device_id=device,
        device_id_type=MESH,
    )


def greet():
    z, y, x, zh, core = place()
    barrier = pltpu.get_barrier_semaphore()
    others = [dev(z, y, x, zh, 1 - core)]
    for step in (1, 2, 3):
        for r in (0, 1):
            others.append(dev((z + step) % 4, y, x, zh, r))
    others += [dev(z, (y + 1) % 4, x, zh, core), dev(z, (y + 3) % 4, x, zh, core)]
    others += [dev(z, y, (x + 1) % 4, zh, core), dev(z, y, (x + 3) % 4, zh, core)]
    others.append(dev(z, y, x, 1 - zh, core))
    for other in others:
        pl.semaphore_signal(barrier, inc=1, device_id=other, device_id_type=MESH)
    pl.semaphore_wait(barrier, len(others))


def slot_table(random_ref, global_ref):
    first = lax.axis_index("seq") * 4
    rows = lax.broadcasted_iota(jnp.int32, (8, 128), 0)
    lanes = lax.broadcasted_iota(jnp.int32, (8, 128), 1)
    table = jnp.zeros((8, 128), jnp.int32)
    for i in range(4):
        own = first + i
        ids = [own - 1, own, own + 1]
        ids += [random_ref[i, t] for t in range(3)]
        ids += [global_ref[t] for t in range(2)]
        for t, block in enumerate(ids):
            dead = jnp.logical_or(block < 0, block > 63)
            for earlier in ids[:t]:
                dead = jnp.logical_or(dead, block == earlier)
            block = jnp.minimum(jnp.maximum(block, 0), 63)
            at = ((block >> 2) & 3) * 32 + ((block >> 1) & 1) * 16 + (block >> 4) * 2 + (block & 1)
            here = rows == i
            table = jnp.where(jnp.logical_and(here, lanes == t), at, table)
            table = jnp.where(
                jnp.logical_and(here, lanes == SLOTS + t), dead.astype(jnp.int32), table
            )
    return table


def gather_kernel(
    q_ref,
    k_ref,
    v_ref,
    dm_ref,
    w_hbm,
    random_ref,
    global_ref,
    tables_ref,
    qm_ref,
    da_ref,
    probs_hbm,
    scores_hbm,
    dq_ref,
    ol_ref,
    w_ref,
    probs_ref,
    scores_ref,
    kv_ref,
    table_ref,
    dm_all,
    grad,
    grad_acc,
    ids_ref,
    outs,
    full,
    kcat,
    vcat,
    id_sem,
    a_send,
    a_recv,
    b_send,
    b_recv,
    y_send,
    y_recv,
    ys_send,
    ys_recv,
    z_send,
    z_recv,
    x_send,
    x_recv,
    xs_send,
    xs_recv,
    g_send,
    g_recv,
    o_send,
    o_recv,
):
    z, y, x, zh, core = place()
    sibling = dev(z, y, x, zh, 1 - core)
    sent = []
    load_w = pltpu.make_async_copy(w_hbm, w_ref, id_sem.at[1])
    load_w.start()
    table_ref[...] = slot_table(random_ref, global_ref)
    greet()

    def send(src, dst, send_sem, recv_sem, device):
        copy = copy_to(src, dst, send_sem, recv_sem, device)
        copy.start()
        sent.append(copy)

    def arrive(dst, recv_sem, send_sem):
        copy_to(dst, dst, send_sem, recv_sem, sibling).wait_recv()

    y_up, y_down = dev(z, (y + 1) % 4, x, zh, core), dev(z, (y + 3) % 4, x, zh, core)
    x_up, x_down = dev(z, y, (x + 1) % 4, zh, core), dev(z, y, (x + 3) % 4, zh, core)
    partner = dev(z, y, x, 1 - zh, core)
    y_of = (y, (y + 3) % 4, (y + 1) % 4, (y + 2) % 4)
    x_of = (x, (x + 3) % 4, (x + 1) % 4, (x + 2) % 4)

    def to_line(src, dst, send_sem, recv_sem, j, r):
        there = 2 * core + j
        here = jnp.logical_and(there == z, core == r)

        @pl.when(here)
        def _():
            pltpu.make_async_copy(src, dst, recv_sem).start()

        @pl.when(jnp.logical_not(here))
        def _():
            copy_to(src, dst, send_sem, recv_sem, dev(there, y, x, zh, r)).start()

    def line_sent(src, dst, send_sem, recv_sem, j, r):
        there = 2 * core + j
        here = jnp.logical_and(there == z, core == r)

        @pl.when(jnp.logical_not(here))
        def _():
            copy_to(src, dst, send_sem, recv_sem, dev(there, y, x, zh, r)).wait_send()

    def piece(src, j, r):
        return src.at[pl.ds(2 * r, 2), :, pl.ds(j * 128, 128)]

    def kv_at(yy, r, t, zz, count):
        return kv_ref.at[pl.ds((((yy * 2 + r) * 2 + t) * 4 + zz) * 2, 2 * count)]

    def kv_args(t):
        for j in (0, 1):
            for r in (0, 1):
                yield (
                    piece((k_ref, v_ref)[t], j, r),
                    kv_at(y, r, t, z, 1),
                    a_send.at[t, j, r],
                    a_recv.at[t, z],
                    j,
                    r,
                )

    def query_args():
        for j in (0, 1):
            for r in (0, 1):
                yield (
                    piece(q_ref, j, r),
                    qm_ref.at[pl.ds(2 * z, 2)],
                    a_send.at[2, j, r],
                    a_recv.at[2, z],
                    j,
                    r,
                )

    def grad_args(r):
        for j in (0, 1):
            yield (
                piece(grad, j, r),
                da_ref.at[pl.ds(2 * z, 2)],
                g_send.at[j, r],
                g_recv.at[z],
                j,
                r,
            )

    def dm_block(wave, slot, late):
        return dm_all.at[wave, core, x_of[slot], (1 - zh) if late else zh]

    def own_rows(wave):
        return dm_ref.at[pl.ds(wave * 256, 256)]

    def dm_to_sibling(wave, slot, late, src):
        k = (1 - zh) if late else zh
        send(
            src,
            dm_block(wave, slot, late),
            xs_send.at[wave, slot, late],
            xs_recv.at[wave, x_of[slot], k],
            sibling,
        )

    def dm_to_ring(wave, late, src):
        dst = dm_block(wave, 0, late)
        send(src, dst, x_send.at[wave, late, 0], x_recv.at[wave, late, 0], x_up)
        send(src, dst, x_send.at[wave, late, 1], x_recv.at[wave, late, 1], x_down)
        dm_to_sibling(wave, 0, late, src)

    def dm_to_partner(wave):
        send(
            own_rows(wave),
            dm_block(wave, 0, 0),
            z_send.at[wave],
            z_recv.at[wave],
            partner,
        )

    def dm_from_partner(wave):
        block = dm_block(wave, 0, 1)
        arrive(block, z_recv.at[wave], z_send.at[wave])
        dm_to_ring(wave, 1, block)

    def dm_from_ring(wave, late):
        for side in (0, 1):
            block = dm_block(wave, 1 + side, late)
            arrive(block, x_recv.at[wave, late, side], x_send.at[wave, late, side])
            if side == (wave + late) % 2:
                send(
                    block,
                    block,
                    x_send.at[wave, late, 2],
                    x_recv.at[wave, late, 2],
                    (x_up, x_down)[side],
                )
            dm_to_sibling(wave, 1 + side, late, block)

    def dm_from_far(wave, late):
        block = dm_block(wave, 3, late)
        arrive(block, x_recv.at[wave, late, 2], x_send.at[wave, late, 2])
        dm_to_sibling(wave, 3, late, block)

    def kv_from_line(t):
        for zz in range(4):
            arrive(kv_at(y, core, t, zz, 1), a_recv.at[t, zz], a_send.at[t, 0, 0])
        own = kv_at(y, core, t, 0, 4)
        send(own, own, y_send.at[t, 0], y_recv.at[t, 0], y_up)
        send(own, own, y_send.at[t, 1], y_recv.at[t, 1], y_down)
        send(own, own, ys_send.at[t, 0], ys_recv.at[t, 0], sibling)

    def kv_from_ring(t):
        for side in (0, 1):
            block = kv_at(y_of[1 + side], core, t, 0, 4)
            arrive(block, y_recv.at[t, side], y_send.at[t, side])
            part = kv_at(y_of[1 + side], core, t, 2 * side, 2)
            send(
                part,
                part,
                y_send.at[t, 2 + side],
                y_recv.at[t, 2 + side],
                (y_up, y_down)[side],
            )
            send(block, block, ys_send.at[t, 1 + side], ys_recv.at[t, 1 + side], sibling)

    def kv_from_far(t):
        for side in (0, 1):
            part = kv_at(y_of[3], core, t, 2 * side, 2)
            arrive(part, y_recv.at[t, 2 + side], y_send.at[t, 2 + side])
        block = kv_at(y_of[3], core, t, 0, 4)
        send(block, block, ys_send.at[t, 3], ys_recv.at[t, 3], sibling)

    def add_product(wave, from_core, fresh):
        if fresh:
            grad_acc[...] = jnp.zeros_like(grad_acc)

        def step(i, carry):
            xx, k = i // 2, i % 2
            at = pl.multiple_of((xx * 4 + k * 2 + from_core) * 256, 256)
            grad_acc[...] += lax.dot_general(
                dm_all[wave, from_core, xx, k],
                w_ref[:, pl.ds(at, 256)],
                CONTRACT_LAST,
                preferred_element_type=F32,
            )
            return carry

        lax.fori_loop(0, 8, step, 0, unroll=True)

    def make_grad(wave):
        add_product(wave, core, True)
        for xx in range(4):
            for k in (0, 1):
                arrive(
                    dm_all.at[wave, 1 - core, xx, k],
                    xs_recv.at[wave, xx, k],
                    xs_send.at[wave, 0, 0],
                )
        add_product(wave, 1 - core, False)
        grad[2 * wave] = grad_acc[:128, :].astype(BF16)
        grad[2 * wave + 1] = grad_acc[128:, :].astype(BF16)
        for args in grad_args(wave):
            to_line(*args)

    for args in kv_args(0):
        to_line(*args)
    dm_to_partner(0)
    for wave in (0, 1):
        dm_to_ring(wave, 0, own_rows(wave))
    for args in kv_args(1):
        to_line(*args)
    dm_to_partner(1)
    for step in (1, 2, 3):
        send(
            table_ref,
            tables_ref.at[z],
            b_send.at[step - 1],
            b_recv.at[step - 1],
            dev((z + step) % 4, y, x, zh, core),
        )
    tables_ref[z] = table_ref[...]
    for wave in (0, 1):
        dm_all[wave, core, x, zh] = dm_ref[wave * 256 : (wave + 1) * 256, :]

    kv_from_line(0)
    dm_from_partner(0)
    dm_from_ring(0, 0)
    dm_from_ring(1, 0)
    kv_from_line(1)
    for args in query_args():
        to_line(*args)
    dm_from_partner(1)
    kv_from_ring(0)
    dm_from_ring(0, 1)
    kv_from_ring(1)
    dm_from_far(0, 0)
    dm_from_far(1, 0)
    dm_from_far(0, 1)
    dm_from_ring(1, 1)
    kv_from_far(0)
    load_w.wait()
    make_grad(0)
    dm_from_far(1, 1)
    kv_from_far(1)
    make_grad(1)

    for step in (1, 2, 3):
        arrive(tables_ref.at[(z - step + 4) % 4], b_recv.at[step - 1], b_send.at[step - 1])
    to_smem = pltpu.make_async_copy(tables_ref, ids_ref, id_sem.at[0])
    to_smem.start()
    for t in (0, 1):
        for slot in range(4):
            arrive(kv_at(y_of[slot], 1 - core, t, 0, 4), ys_recv.at[t, slot], ys_send.at[t, 0])
    for zz in range(4):
        arrive(qm_ref.at[pl.ds(2 * zz, 2)], a_recv.at[2, zz], a_send.at[2, 0, 0])
    to_smem.wait()

    scale = HEAD_DIM ** (-0.5)

    def forward(n, carry):
        zz, i = n // 2, 2 * core + n % 2
        for t in range(SLOTS):
            at = ids_ref[zz, i, t]
            kcat[n, t * BLOCK : (t + 1) * BLOCK, :] = kv_ref[at]
            vcat[n, t * BLOCK : (t + 1) * BLOCK, :] = kv_ref[at + 8]
        bias = jnp.concatenate(
            [
                jnp.full((1, BLOCK), ids_ref[zz, i, SLOTS + t].astype(F32) * MASKED, F32)
                for t in range(SLOTS)
            ],
            axis=1,
        )
        scores = (
            lax.dot_general(qm_ref[n], kcat[n], CONTRACT_LAST, preferred_element_type=F32)
            * scale
            + bias
        )
        top = jnp.max(scores, axis=1, keepdims=True)
        powers = jnp.exp(scores - top)
        probs = powers * (1.0 / jnp.sum(powers, axis=1, keepdims=True))
        full[n] = probs
        half = probs.astype(BF16)
        probs_ref[n] = half
        outs[n] = jnp.dot(half, vcat[n], preferred_element_type=F32).astype(BF16)
        return carry

    lax.fori_loop(0, 8, forward, 0, unroll=4)
    keep_probs = pltpu.make_async_copy(probs_ref, probs_hbm, id_sem.at[2])
    keep_probs.start()

    def out_here(zz):
        return jnp.logical_and(z == zz, z // 2 == core)

    def out_piece(zz):
        return outs.at[pl.ds(2 * zz, 2)]

    def out_copy(zz):
        return copy_to(
            out_piece(zz),
            ol_ref.at[z % 2, core],
            o_send.at[zz],
            o_recv.at[z % 2, core],
            dev(zz, y, x, zh, z // 2),
        )

    for zz in range(4):

        @pl.when(out_here(zz))
        def _():
            pltpu.make_async_copy(
                out_piece(zz), ol_ref.at[z % 2, core], o_recv.at[z % 2, core]
            ).start()

        @pl.when(jnp.logical_not(out_here(zz)))
        def _():
            out_copy(zz).start()

    for zz in range(4):
        arrive(da_ref.at[pl.ds(2 * zz, 2)], g_recv.at[zz], g_send.at[0, 0])

    def backward(n, carry):
        grad_rows = da_ref[n]
        delta = jnp.sum(outs[n].astype(F32) * grad_rows.astype(F32), axis=1, keepdims=True)
        prob_grad = lax.dot_general(
            grad_rows, vcat[n], CONTRACT_LAST, preferred_element_type=F32
        )
        score_grad = (full[n] * (prob_grad - delta) * scale).astype(BF16)
        scores_ref[n] = score_grad
        dq_ref[n] = jnp.dot(score_grad, kcat[n], preferred_element_type=F32).astype(BF16)
        return carry

    lax.fori_loop(0, 8, backward, 0, unroll=4)
    keep_scores = pltpu.make_async_copy(scores_ref, scores_hbm, id_sem.at[3])
    keep_scores.start()

    for j in (0, 1):
        for r in (0, 1):
            arrive(ol_ref.at[j, r], o_recv.at[j, r], o_send.at[0])
    for t in (0, 1):
        for args in kv_args(t):
            line_sent(*args)
        for args in grad_args(t):
            line_sent(*args)
    for args in query_args():
        line_sent(*args)
    for zz in range(4):

        @pl.when(jnp.logical_not(out_here(zz)))
        def _():
            out_copy(zz).wait_send()

    for copy in sent:
        copy.wait_send()
    keep_probs.wait()
    keep_scores.wait()


def gather(q, k, v, dm, w, random_blocks, global_blocks):
    vmem = pl.BlockSpec(memory_space=pltpu.VMEM)
    smem = pl.BlockSpec(memory_space=pltpu.SMEM)
    hbm = pl.BlockSpec(memory_space=pl.ANY)
    dma = pltpu.SemaphoreType.DMA
    blocks = jax.ShapeDtypeStruct((8, BLOCK, HEAD_DIM), BF16)
    weights = jax.ShapeDtypeStruct((8, BLOCK, SLOTS * BLOCK), BF16)
    return pl.pallas_call(
        gather_kernel,
        out_shape=(
            jax.ShapeDtypeStruct((4, 8, 128), jnp.int32),
            blocks,
            blocks,
            weights,
            weights,
            blocks,
            jax.ShapeDtypeStruct((2, 2, 2, BLOCK, HEAD_DIM), BF16),
        ),
        in_specs=[vmem] * 4 + [hbm] + [smem] * 2,
        out_specs=(vmem, vmem, vmem, hbm, hbm, vmem, vmem),
        scratch_shapes=[
            pltpu.VMEM((256, 4096), BF16),
            pltpu.VMEM((8, BLOCK, SLOTS * BLOCK), BF16),
            pltpu.VMEM((8, BLOCK, SLOTS * BLOCK), BF16),
            pltpu.VMEM((128, BLOCK, HEAD_DIM), BF16),
            pltpu.VMEM((8, 128), jnp.int32),
            pltpu.VMEM((2, 2, 4, 2, 256, 256), BF16),
            pltpu.VMEM((4, BLOCK, 256), BF16),
            pltpu.VMEM((256, 256), F32),
            pltpu.SMEM((4, 8, 128), jnp.int32),
            pltpu.VMEM((8, BLOCK, HEAD_DIM), BF16),
            pltpu.VMEM((8, BLOCK, SLOTS * BLOCK), F32),
            pltpu.VMEM((8, SLOTS * BLOCK, HEAD_DIM), BF16),
            pltpu.VMEM((8, SLOTS * BLOCK, HEAD_DIM), BF16),
            dma((4,)),
            dma((3, 2, 2)),
            dma((3, 4)),
            dma((3,)),
            dma((3,)),
            dma((2, 4)),
            dma((2, 4)),
            dma((2, 4)),
            dma((2, 4)),
            dma((2,)),
            dma((2,)),
            dma((2, 2, 3)),
            dma((2, 2, 3)),
            dma((2, 4, 2)),
            dma((2, 4, 2)),
            dma((2, 2)),
            dma((4,)),
            dma((4,)),
            dma((2, 2)),
        ],
        compiler_params=pltpu.CompilerParams(
            collective_id=0, has_side_effects=True, vmem_limit_bytes=VMEM_LIMIT
        ),
        name="gather_heads",
    )(q, k, v, dm, w, random_blocks, global_blocks)


def key_grads_kernel(
    ids_ref, q_ref, da_ref, probs_hbm, scores_hbm, dkv_hbm, acc, probs_ref, scores_ref, half, sems, out_sems
):
    core = place()[4]

    def load(part):
        rows = pl.ds(4 * part, 4)
        return (
            pltpu.make_async_copy(
                scores_hbm.at[rows], scores_ref.at[rows], sems.at[part, 0]
            ),
            pltpu.make_async_copy(probs_hbm.at[rows], probs_ref.at[rows], sems.at[part, 1]),
        )

    for part in (0, 1):
        for copy in load(part):
            copy.start()

    def clear(i, carry):
        acc[i] = jnp.zeros((BLOCK, HEAD_DIM), F32)
        return carry

    lax.fori_loop(0, 128, clear, 0, unroll=8)

    def one(n, carry):
        key_add = lax.dot_general(
            scores_ref[n], q_ref[n], CONTRACT_FIRST, preferred_element_type=F32
        )
        value_add = lax.dot_general(
            probs_ref[n], da_ref[n], CONTRACT_FIRST, preferred_element_type=F32
        )
        for t in range(SLOTS):
            at = ids_ref[n // 2, 2 * core + n % 2, t]
            acc[at] += key_add[t * BLOCK : (t + 1) * BLOCK, :]
            acc[at + 8] += value_add[t * BLOCK : (t + 1) * BLOCK, :]
        return carry

    for part in (0, 1):
        for copy in load(part):
            copy.wait()
        lax.fori_loop(4 * part, 4 * part + 4, one, 0, unroll=2)

    def store(part):
        rows = pl.ds(16 * part, 16)
        return pltpu.make_async_copy(half.at[rows], dkv_hbm.at[rows], out_sems.at[part])

    for part in range(8):

        def finish(i, carry):
            half[i] = acc[i].astype(BF16)
            return carry

        lax.fori_loop(16 * part, 16 * part + 16, finish, 0, unroll=8)
        store(part).start()
    for part in range(8):
        store(part).wait()


def key_grads(ids, q, da, probs, scores):
    vmem = pl.BlockSpec(memory_space=pltpu.VMEM)
    smem = pl.BlockSpec(memory_space=pltpu.SMEM)
    hbm = pl.BlockSpec(memory_space=pl.ANY)
    dma = pltpu.SemaphoreType.DMA
    return pl.pallas_call(
        key_grads_kernel,
        out_shape=jax.ShapeDtypeStruct((128, BLOCK, HEAD_DIM), BF16),
        in_specs=[smem, vmem, vmem, hbm, hbm],
        out_specs=hbm,
        scratch_shapes=[
            pltpu.VMEM((128, BLOCK, HEAD_DIM), F32),
            pltpu.VMEM((8, BLOCK, SLOTS * BLOCK), BF16),
            pltpu.VMEM((8, BLOCK, SLOTS * BLOCK), BF16),
            pltpu.VMEM((128, BLOCK, HEAD_DIM), BF16),
            dma((2, 2)),
            dma((8,)),
        ],
        compiler_params=pltpu.CompilerParams(vmem_limit_bytes=VMEM_LIMIT),
        name="key_grads",
    )(ids, q, da, probs, scores)


def unpack(pieces, out_ref):
    for j in (0, 1):
        for r in (0, 1):
            for low in (0, 1):
                row = (2 * r + low) * BLOCK
                out_ref[row : row + BLOCK, j * 128 : (j + 1) * 128] = pieces[j, r, low]


def scatter_kernel(
    ol_ref,
    dq_ref,
    p_hbm,
    w_hbm,
    mixed_ref,
    lands,
    w_ref,
    p_ref,
    load_sems,
    attn,
    terms,
    terms_in,
    xa,
    xc,
    total,
    zb,
    parts,
    parts_in,
    ya,
    yc,
    final,
    l_send,
    l_recv,
    ps_send,
    ps_recv,
    y_send,
    y_recv,
    xs_send,
    xs_recv,
    x_send,
    x_recv,
    z_send,
    z_recv,
):
    z, y, x, zh, core = place()
    sibling = dev(z, y, x, zh, 1 - core)
    sent = []
    load_w = pltpu.make_async_copy(w_hbm, w_ref, load_sems.at[0])
    load_p = pltpu.make_async_copy(p_hbm.at[:, core], p_ref, load_sems.at[1])
    load_w.start()
    load_p.start()
    unpack(ol_ref, attn)
    greet()

    def send(src, dst, send_sem, recv_sem, device):
        copy = copy_to(src, dst, send_sem, recv_sem, device)
        copy.start()
        sent.append(copy)

    def arrive(dst, recv_sem, send_sem):
        copy_to(dst, dst, send_sem, recv_sem, sibling).wait_recv()

    y_dev = (dev(z, (y + 1) % 4, x, zh, core), dev(z, (y + 3) % 4, x, zh, core))
    x_dev = (dev(z, y, (x + 1) % 4, zh, core), dev(z, y, (x + 3) % 4, zh, core))
    y_of = ((y + 2) % 4, (y + 1) % 4, (y + 3) % 4, y)
    x_of = ((x + 2) % 4, (x + 1) % 4, (x + 3) % 4, x)

    def back(u, zz, src):
        dst = lands.at[0, z % 2, core] if u == 0 else grad_land(u - 1, z % 2, core)
        return src, dst, l_send.at[u, zz], l_recv.at[u, z % 2, core], zz

    def start_back(src, dst, send_sem, recv_sem, zz):
        here = jnp.logical_and(z == zz, z // 2 == core)

        @pl.when(here)
        def _():
            pltpu.make_async_copy(src, dst, recv_sem).start()

        @pl.when(jnp.logical_not(here))
        def _():
            copy_to(src, dst, send_sem, recv_sem, dev(zz, y, x, zh, z // 2)).start()

    def sent_back(src, dst, send_sem, recv_sem, zz):
        here = jnp.logical_and(z == zz, z // 2 == core)

        @pl.when(jnp.logical_not(here))
        def _():
            copy_to(src, dst, send_sem, recv_sem, dev(zz, y, x, zh, z // 2)).wait_send()

    def landed(u):
        for j in (0, 1):
            for r in (0, 1):
                dst = lands.at[0, j, r] if u == 0 else grad_land(u - 1, j, r)
                arrive(dst, l_recv.at[u, j, r], l_send.at[u, 0])

    def grad_land(u, j, r):
        return lands.at[1 + u // 2, j, r, u % 2]

    def query_piece(zz):
        return dq_ref.at[pl.ds(2 * zz, 2)]

    def parts_to_sibling(t):
        for n in range(4):
            send(
                p_hbm.at[y_of[n], 1 - core, t // 2, :, t % 2],
                parts_in.at[t, n],
                ps_send.at[t, n],
                ps_recv.at[t, n],
                sibling,
            )

    def add_parts(t, n, zz, more):
        value = p_ref[y_of[n], t // 2, zz, t % 2].astype(F32) + parts_in[t, n, zz].astype(F32)
        for ref in more:
            value += ref.astype(F32)
        return value.astype(BF16)

    def parts_here(t, n):
        arrive(parts_in.at[t, n], ps_recv.at[t, n], ps_send.at[t, n])

    def parts_far(t):
        parts_here(t, 0)
        for side in (0, 1):
            for zz in (2 * side, 2 * side + 1):
                parts[t, 0, zz] = add_parts(t, 0, zz, ())
            send(
                parts.at[t, 0, pl.ds(2 * side, 2)],
                ya.at[t, side],
                y_send.at[t, side],
                y_recv.at[t, side],
                y_dev[side],
            )

    def parts_near(t):
        for side in (0, 1):
            n = 1 + side
            parts_here(t, n)
            for zz in (2 - 2 * side, 3 - 2 * side):
                parts[t, n, zz] = add_parts(t, n, zz, ())
            arrive(ya.at[t, side], y_recv.at[t, side], y_send.at[t, side])
            for low in (0, 1):
                zz = 2 * side + low
                parts[t, n, zz] = add_parts(t, n, zz, (ya[t, side, low],))
            send(
                parts.at[t, n],
                yc.at[t, side],
                y_send.at[t, n + 1],
                y_recv.at[t, n + 1],
                y_dev[side],
            )

    def parts_end(t):
        parts_here(t, 3)
        for side in (0, 1):
            arrive(yc.at[t, side], y_recv.at[t, 2 + side], y_send.at[t, 2 + side])
        for zz in range(4):
            final[t, zz] = add_parts(t, 3, zz, (yc[t, 0, zz], yc[t, 1, zz]))
            start_back(*back(1 + t, zz, final.at[t, zz]))

    def make_terms(wave, to_core, n):
        for k in (0, 1):
            at = pl.multiple_of((x_of[n] * 4 + k * 2 + to_core) * 256, 256)
            terms[wave, to_core, n, k] = jnp.dot(
                attn[wave * 128 : (wave + 1) * 128, :],
                w_ref[:, pl.ds(at, 256)],
                preferred_element_type=F32,
            ).astype(BF16)

    def terms_to_sibling(wave):
        for n in range(4):
            make_terms(wave, 1 - core, n)
            send(
                terms.at[wave, 1 - core, n],
                terms_in.at[wave, n],
                xs_send.at[wave, n],
                xs_recv.at[wave, n],
                sibling,
            )

    def terms_here(wave, n):
        make_terms(wave, core, n)
        arrive(terms_in.at[wave, n], xs_recv.at[wave, n], xs_send.at[wave, n])

    def add_terms(wave, n, k, more):
        value = terms[wave, core, n, k].astype(F32) + terms_in[wave, n, k].astype(F32)
        for ref in more:
            value += ref.astype(F32)
        return value.astype(BF16)

    def terms_far(wave):
        terms_here(wave, 0)
        for k in (0, 1):
            terms[wave, core, 0, k] = add_terms(wave, 0, k, ())
            send(
                terms.at[wave, core, 0, k],
                xa.at[wave, k],
                x_send.at[wave, k],
                x_recv.at[wave, k],
                x_dev[k],
            )

    def terms_near(wave):
        for side in (0, 1):
            n = 1 + side
            terms_here(wave, n)
            arrive(xa.at[wave, side], x_recv.at[wave, side], x_send.at[wave, side])
            terms[wave, core, n, side] = add_terms(wave, n, side, (xa[wave, side],))
            terms[wave, core, n, 1 - side] = add_terms(wave, n, 1 - side, ())
            send(
                terms.at[wave, core, n],
                xc.at[wave, side],
                x_send.at[wave, n + 1],
                x_recv.at[wave, n + 1],
                x_dev[side],
            )

    def terms_end(wave):
        terms_here(wave, 3)
        for side in (0, 1):
            arrive(xc.at[wave, side], x_recv.at[wave, 2 + side], x_send.at[wave, 2 + side])

        def add_total(k):
            total[wave, k] = add_terms(wave, 3, k, (xc[wave, 0, k], xc[wave, 1, k]))

        add_total(1 - zh)
        send(
            total.at[wave, 1 - zh],
            zb.at[wave],
            z_send.at[wave],
            z_recv.at[wave],
            dev(z, y, x, 1 - zh, core),
        )
        add_total(zh)

    def mixed_end(wave):
        arrive(zb.at[wave], z_recv.at[wave], z_send.at[wave])
        mixed_ref[wave * 128 : (wave + 1) * 128, :] = (
            total[wave, zh].astype(F32) + zb[wave].astype(F32)
        ).astype(BF16)

    parts_to_sibling(0)
    parts_to_sibling(1)
    for zz in range(4):
        start_back(*back(0, zz, query_piece(zz)))
    load_w.wait()
    terms_to_sibling(0)
    load_p.wait()
    parts_far(0)
    parts_to_sibling(2)
    terms_to_sibling(1)
    terms_far(0)
    parts_far(1)
    parts_to_sibling(3)
    terms_to_sibling(2)
    parts_near(0)
    terms_far(1)
    parts_far(2)
    terms_to_sibling(3)
    terms_near(0)
    parts_near(1)
    terms_far(2)
    parts_far(3)
    parts_end(0)
    terms_near(1)
    parts_near(2)
    terms_far(3)
    terms_end(0)
    parts_end(1)
    terms_near(2)
    parts_near(3)
    terms_end(1)
    parts_end(2)
    terms_near(3)
    terms_end(2)
    parts_end(3)
    terms_end(3)
    for wave in range(4):
        mixed_end(wave)
    for u in range(5):
        landed(u)
    for zz in range(4):
        sent_back(*back(0, zz, query_piece(zz)))
        for t in range(4):
            sent_back(*back(1 + t, zz, final.at[t, zz]))
    for copy in sent:
        copy.wait_send()


def scatter(ol, dq, dkv, w):
    vmem = pl.BlockSpec(memory_space=pltpu.VMEM)
    hbm = pl.BlockSpec(memory_space=pl.ANY)
    dma = pltpu.SemaphoreType.DMA
    return pl.pallas_call(
        scatter_kernel,
        out_shape=(
            jax.ShapeDtypeStruct((512, 256), BF16),
            jax.ShapeDtypeStruct((3, 2, 2, 2, BLOCK, HEAD_DIM), BF16),
        ),
        in_specs=[vmem, vmem, hbm, hbm],
        out_specs=(vmem,) * 2,
        scratch_shapes=[
            pltpu.VMEM((256, 4096), BF16),
            pltpu.VMEM((4, 2, 4, 2, BLOCK, HEAD_DIM), BF16),
            dma((2,)),
            pltpu.VMEM((512, 256), BF16),
            pltpu.VMEM((4, 2, 4, 2, 128, 256), BF16),
            pltpu.VMEM((4, 4, 2, 128, 256), BF16),
            pltpu.VMEM((4, 2, 128, 256), BF16),
            pltpu.VMEM((4, 2, 2, 128, 256), BF16),
            pltpu.VMEM((4, 2, 128, 256), BF16),
            pltpu.VMEM((4, 128, 256), BF16),
            pltpu.VMEM((4, 4, 4, BLOCK, HEAD_DIM), BF16),
            pltpu.VMEM((4, 4, 4, BLOCK, HEAD_DIM), BF16),
            pltpu.VMEM((4, 2, 2, BLOCK, HEAD_DIM), BF16),
            pltpu.VMEM((4, 2, 4, BLOCK, HEAD_DIM), BF16),
            pltpu.VMEM((4, 4, BLOCK, HEAD_DIM), BF16),
            dma((5, 4)),
            dma((5, 2, 2)),
            dma((4, 4)),
            dma((4, 4)),
            dma((4, 4)),
            dma((4, 4)),
            dma((4, 4)),
            dma((4, 4)),
            dma((4, 4)),
            dma((4, 4)),
            dma((4,)),
            dma((4,)),
        ],
        compiler_params=pltpu.CompilerParams(
            collective_id=1, has_side_effects=True, vmem_limit_bytes=VMEM_LIMIT
        ),
        name="scatter_heads",
    )(ol, dq, dkv, w)


def unpack_kernel(mixed_ref, lands_ref, mixed_out, dq_out, dk_out, dv_out):
    mixed_out[...] = mixed_ref[...]
    unpack(lands_ref.at[0], dq_out)
    unpack(lands_ref.at[1], dk_out)
    unpack(lands_ref.at[2], dv_out)


def unpack_all(mixed, lands):
    vmem = pl.BlockSpec(memory_space=pltpu.VMEM)
    return pl.pallas_call(
        unpack_kernel,
        out_shape=(jax.ShapeDtypeStruct((512, 256), BF16),) * 4,
        in_specs=[vmem] * 2,
        out_specs=(vmem,) * 4,
        name="unpack_outputs",
    )(mixed, lands)


def body(queries, keys, values, w_out, d_mixed, random_blocks, global_blocks):
    by_block = (4, BLOCK, 2 * HEAD_DIM)
    ids, q, da, probs, scores, dq, ol = gather(
        queries.reshape(by_block),
        keys.reshape(by_block),
        values.reshape(by_block),
        d_mixed,
        w_out,
        random_blocks,
        global_blocks,
    )
    dkv = key_grads(ids, q, da, probs, scores)
    dkv = dkv.reshape(4, 2, 2, 4, 2, BLOCK, HEAD_DIM)
    return unpack_all(*scatter(ol, dq, dkv, w_out))


def solution(mesh):
    return jax.shard_map(
        body,
        mesh=mesh,
        in_specs=(
            P("seq", "head"),
            P("seq", "head"),
            P("seq", "head"),
            P("head", None),
            P("seq", "head"),
            P("seq", None),
            P(),
        ),
        out_specs=(P("seq", "head"), P("seq", "head"), P("seq", "head"), P("seq", "head")),
        check_vma=False,
    )
```

```python
import jax
import jax.numpy as jnp
from jax import lax
from jax.experimental import pallas as pl
from jax.experimental.pallas import tpu as pltpu
from jax.sharding import PartitionSpec as P

HEAD_DIM = 128
BLOCK = 128
SLOTS = 8
MASKED = -1e30
CONTRACT_LAST = (((1,), (1,)), ((), ()))
CONTRACT_FIRST = (((0,), (0,)), ((), ()))
MESH = pl.DeviceIdType.MESH
BF16 = jnp.bfloat16
F32 = jnp.float32
VMEM_LIMIT = 56 * 1024 * 1024


def place():
    seq, head = lax.axis_index("seq"), lax.axis_index("head")
    return seq // 4, seq % 4, head // 4, (head // 2) % 2, head % 2


def dev(z, y, x, zh, core):
    return (z * 4 + y, x * 4 + zh * 2 + core)


def copy_to(src, dst, send_sem, recv_sem, device):
    return pltpu.make_async_remote_copy(
        src_ref=src,
        dst_ref=dst,
        send_sem=send_sem,
        recv_sem=recv_sem,
        device_id=device,
        device_id_type=MESH,
    )


def greet():
    z, y, x, zh, core = place()
    barrier = pltpu.get_barrier_semaphore()
    others = [dev(z, y, x, zh, 1 - core)]
    for step in (1, 2, 3):
        for r in (0, 1):
            others.append(dev((z + step) % 4, y, x, zh, r))
    others += [dev(z, (y + 1) % 4, x, zh, core), dev(z, (y + 3) % 4, x, zh, core)]
    others += [dev(z, y, (x + 1) % 4, zh, core), dev(z, y, (x + 3) % 4, zh, core)]
    others.append(dev(z, y, x, 1 - zh, core))
    for other in others:
        pl.semaphore_signal(barrier, inc=1, device_id=other, device_id_type=MESH)
    pl.semaphore_wait(barrier, len(others))


def slot_table(random_ref, global_ref):
    first = lax.axis_index("seq") * 4
    rows = lax.broadcasted_iota(jnp.int32, (8, 128), 0)
    lanes = lax.broadcasted_iota(jnp.int32, (8, 128), 1)
    table = jnp.zeros((8, 128), jnp.int32)
    for i in range(4):
        own = first + i
        ids = [own - 1, own, own + 1]
        ids += [random_ref[i, t] for t in range(3)]
        ids += [global_ref[t] for t in range(2)]
        for t, block in enumerate(ids):
            dead = jnp.logical_or(block < 0, block > 63)
            for earlier in ids[:t]:
                dead = jnp.logical_or(dead, block == earlier)
            block = jnp.minimum(jnp.maximum(block, 0), 63)
            at = ((block >> 2) & 3) * 32 + ((block >> 1) & 1) * 16 + (block >> 4) * 2 + (block & 1)
            here = rows == i
            table = jnp.where(jnp.logical_and(here, lanes == t), at, table)
            table = jnp.where(
                jnp.logical_and(here, lanes == SLOTS + t), dead.astype(jnp.int32), table
            )
    return table


def gather_kernel(
    q_ref,
    k_ref,
    v_ref,
    dm_ref,
    w_hbm,
    random_ref,
    global_ref,
    tables_ref,
    qm_ref,
    da_ref,
    probs_hbm,
    scores_hbm,
    dq_ref,
    ol_ref,
    w_ref,
    probs_ref,
    scores_ref,
    kv_ref,
    table_ref,
    dm_all,
    grad,
    grad_acc,
    ids_ref,
    outs,
    full,
    kcat,
    vcat,
    id_sem,
    a_send,
    a_recv,
    b_send,
    b_recv,
    y_send,
    y_recv,
    ys_send,
    ys_recv,
    z_send,
    z_recv,
    x_send,
    x_recv,
    xs_send,
    xs_recv,
    g_send,
    g_recv,
    o_send,
    o_recv,
):
    z, y, x, zh, core = place()
    sibling = dev(z, y, x, zh, 1 - core)
    sent = []
    load_w = pltpu.make_async_copy(w_hbm, w_ref, id_sem.at[1])
    load_w.start()
    table_ref[...] = slot_table(random_ref, global_ref)
    greet()

    def send(src, dst, send_sem, recv_sem, device):
        copy = copy_to(src, dst, send_sem, recv_sem, device)
        copy.start()
        sent.append(copy)

    def arrive(dst, recv_sem, send_sem):
        copy_to(dst, dst, send_sem, recv_sem, sibling).wait_recv()

    y_up, y_down = dev(z, (y + 1) % 4, x, zh, core), dev(z, (y + 3) % 4, x, zh, core)
    x_up, x_down = dev(z, y, (x + 1) % 4, zh, core), dev(z, y, (x + 3) % 4, zh, core)
    partner = dev(z, y, x, 1 - zh, core)
    y_of = (y, (y + 3) % 4, (y + 1) % 4, (y + 2) % 4)
    x_of = (x, (x + 3) % 4, (x + 1) % 4, (x + 2) % 4)

    def to_line(src, dst, send_sem, recv_sem, j, r):
        there = 2 * core + j
        here = jnp.logical_and(there == z, core == r)

        @pl.when(here)
        def _():
            pltpu.make_async_copy(src, dst, recv_sem).start()

        @pl.when(jnp.logical_not(here))
        def _():
            copy_to(src, dst, send_sem, recv_sem, dev(there, y, x, zh, r)).start()

    def line_sent(src, dst, send_sem, recv_sem, j, r):
        there = 2 * core + j
        here = jnp.logical_and(there == z, core == r)

        @pl.when(jnp.logical_not(here))
        def _():
            copy_to(src, dst, send_sem, recv_sem, dev(there, y, x, zh, r)).wait_send()

    def piece(src, j, r):
        return src.at[pl.ds(2 * r, 2), :, pl.ds(j * 128, 128)]

    def kv_at(yy, r, t, zz, count):
        return kv_ref.at[pl.ds((((yy * 2 + r) * 2 + t) * 4 + zz) * 2, 2 * count)]

    def kv_args(t):
        for j in (0, 1):
            for r in (0, 1):
                yield (
                    piece((k_ref, v_ref)[t], j, r),
                    kv_at(y, r, t, z, 1),
                    a_send.at[t, j, r],
                    a_recv.at[t, z],
                    j,
                    r,
                )

    def query_args():
        for j in (0, 1):
            for r in (0, 1):
                yield (
                    piece(q_ref, j, r),
                    qm_ref.at[pl.ds(2 * z, 2)],
                    a_send.at[2, j, r],
                    a_recv.at[2, z],
                    j,
                    r,
                )

    def grad_args(r):
        for j in (0, 1):
            yield (
                piece(grad, j, r),
                da_ref.at[pl.ds(2 * z, 2)],
                g_send.at[j, r],
                g_recv.at[z],
                j,
                r,
            )

    def dm_block(wave, slot, late):
        return dm_all.at[wave, core, x_of[slot], (1 - zh) if late else zh]

    def own_rows(wave):
        return dm_ref.at[pl.ds(wave * 256, 256)]

    def dm_to_sibling(wave, slot, late, src):
        k = (1 - zh) if late else zh
        send(
            src,
            dm_block(wave, slot, late),
            xs_send.at[wave, slot, late],
            xs_recv.at[wave, x_of[slot], k],
            sibling,
        )

    def dm_to_ring(wave, late, src):
        dst = dm_block(wave, 0, late)
        send(src, dst, x_send.at[wave, late, 0], x_recv.at[wave, late, 0], x_up)
        send(src, dst, x_send.at[wave, late, 1], x_recv.at[wave, late, 1], x_down)
        dm_to_sibling(wave, 0, late, src)

    def dm_to_partner(wave):
        send(
            own_rows(wave),
            dm_block(wave, 0, 0),
            z_send.at[wave],
            z_recv.at[wave],
            partner,
        )

    def dm_from_partner(wave):
        block = dm_block(wave, 0, 1)
        arrive(block, z_recv.at[wave], z_send.at[wave])
        dm_to_ring(wave, 1, block)

    def dm_from_ring(wave, late):
        for side in (0, 1):
            block = dm_block(wave, 1 + side, late)
            arrive(block, x_recv.at[wave, late, side], x_send.at[wave, late, side])
            if side == (wave + late) % 2:
                send(
                    block,
                    block,
                    x_send.at[wave, late, 2],
                    x_recv.at[wave, late, 2],
                    (x_up, x_down)[side],
                )
            dm_to_sibling(wave, 1 + side, late, block)

    def dm_from_far(wave, late):
        block = dm_block(wave, 3, late)
        arrive(block, x_recv.at[wave, late, 2], x_send.at[wave, late, 2])
        dm_to_sibling(wave, 3, late, block)

    def kv_from_line(t):
        for zz in range(4):
            arrive(kv_at(y, core, t, zz, 1), a_recv.at[t, zz], a_send.at[t, 0, 0])
        own = kv_at(y, core, t, 0, 4)
        send(own, own, y_send.at[t, 0], y_recv.at[t, 0], y_up)
        send(own, own, y_send.at[t, 1], y_recv.at[t, 1], y_down)
        send(own, own, ys_send.at[t, 0], ys_recv.at[t, 0], sibling)

    def kv_from_ring(t):
        for side in (0, 1):
            block = kv_at(y_of[1 + side], core, t, 0, 4)
            arrive(block, y_recv.at[t, side], y_send.at[t, side])
            part = kv_at(y_of[1 + side], core, t, 2 * side, 2)
            send(
                part,
                part,
                y_send.at[t, 2 + side],
                y_recv.at[t, 2 + side],
                (y_up, y_down)[side],
            )
            send(block, block, ys_send.at[t, 1 + side], ys_recv.at[t, 1 + side], sibling)

    def kv_from_far(t):
        for side in (0, 1):
            part = kv_at(y_of[3], core, t, 2 * side, 2)
            arrive(part, y_recv.at[t, 2 + side], y_send.at[t, 2 + side])
        block = kv_at(y_of[3], core, t, 0, 4)
        send(block, block, ys_send.at[t, 3], ys_recv.at[t, 3], sibling)

    def add_product(wave, from_core, fresh):
        if fresh:
            grad_acc[...] = jnp.zeros_like(grad_acc)

        def step(i, carry):
            xx, k = i // 2, i % 2
            at = pl.multiple_of((xx * 4 + k * 2 + from_core) * 256, 256)
            grad_acc[...] += lax.dot_general(
                dm_all[wave, from_core, xx, k],
                w_ref[:, pl.ds(at, 256)],
                CONTRACT_LAST,
                preferred_element_type=F32,
            )
            return carry

        lax.fori_loop(0, 8, step, 0, unroll=True)

    def make_grad(wave):
        add_product(wave, core, True)
        for xx in range(4):
            for k in (0, 1):
                arrive(
                    dm_all.at[wave, 1 - core, xx, k],
                    xs_recv.at[wave, xx, k],
                    xs_send.at[wave, 0, 0],
                )
        add_product(wave, 1 - core, False)
        grad[2 * wave] = grad_acc[:128, :].astype(BF16)
        grad[2 * wave + 1] = grad_acc[128:, :].astype(BF16)
        for args in grad_args(wave):
            to_line(*args)

    dm_to_partner(0)
    for args in kv_args(0):
        to_line(*args)
    for wave in (0, 1):
        dm_to_ring(wave, 0, own_rows(wave))
    dm_to_partner(1)
    for args in kv_args(1):
        to_line(*args)
    for step in (1, 2, 3):
        send(
            table_ref,
            tables_ref.at[z],
            b_send.at[step - 1],
            b_recv.at[step - 1],
            dev((z + step) % 4, y, x, zh, core),
        )
    tables_ref[z] = table_ref[...]
    for wave in (0, 1):
        dm_all[wave, core, x, zh] = dm_ref[wave * 256 : (wave + 1) * 256, :]

    kv_from_line(0)
    dm_from_partner(0)
    dm_from_ring(0, 0)
    dm_from_ring(1, 0)
    kv_from_line(1)
    for args in query_args():
        to_line(*args)
    dm_from_partner(1)
    kv_from_ring(0)
    dm_from_ring(0, 1)
    kv_from_ring(1)
    dm_from_far(0, 0)
    dm_from_far(1, 0)
    dm_from_far(0, 1)
    dm_from_ring(1, 1)
    kv_from_far(0)
    load_w.wait()
    make_grad(0)
    dm_from_far(1, 1)
    kv_from_far(1)
    make_grad(1)

    for step in (1, 2, 3):
        arrive(tables_ref.at[(z - step + 4) % 4], b_recv.at[step - 1], b_send.at[step - 1])
    to_smem = pltpu.make_async_copy(tables_ref, ids_ref, id_sem.at[0])
    to_smem.start()
    for t in (0, 1):
        for slot in range(4):
            arrive(kv_at(y_of[slot], 1 - core, t, 0, 4), ys_recv.at[t, slot], ys_send.at[t, 0])
    for zz in range(4):
        arrive(qm_ref.at[pl.ds(2 * zz, 2)], a_recv.at[2, zz], a_send.at[2, 0, 0])
    to_smem.wait()

    scale = HEAD_DIM ** (-0.5)

    def forward(n, carry):
        zz, i = n // 2, 2 * core + n % 2
        for t in range(SLOTS):
            at = ids_ref[zz, i, t]
            kcat[n, t * BLOCK : (t + 1) * BLOCK, :] = kv_ref[at]
            vcat[n, t * BLOCK : (t + 1) * BLOCK, :] = kv_ref[at + 8]
        bias = jnp.concatenate(
            [
                jnp.full((1, BLOCK), ids_ref[zz, i, SLOTS + t].astype(F32) * MASKED, F32)
                for t in range(SLOTS)
            ],
            axis=1,
        )
        scores = (
            lax.dot_general(qm_ref[n], kcat[n], CONTRACT_LAST, preferred_element_type=F32)
            * scale
            + bias
        )
        top = jnp.max(scores, axis=1, keepdims=True)
        powers = jnp.exp(scores - top)
        probs = powers * (1.0 / jnp.sum(powers, axis=1, keepdims=True))
        full[n] = probs
        half = probs.astype(BF16)
        probs_ref[n] = half
        outs[n] = jnp.dot(half, vcat[n], preferred_element_type=F32).astype(BF16)
        return carry

    def out_here(zz):
        return jnp.logical_and(z == zz, z // 2 == core)

    def out_piece(zz):
        return outs.at[pl.ds(2 * zz, 2)]

    def out_copy(zz):
        return copy_to(
            out_piece(zz),
            ol_ref.at[z % 2, core],
            o_send.at[zz],
            o_recv.at[z % 2, core],
            dev(zz, y, x, zh, z // 2),
        )

    for zz in range(4):
        if zz % 2 == 0:
            lax.fori_loop(2 * zz, 2 * zz + 4, forward, 0, unroll=4)

        @pl.when(out_here(zz))
        def _():
            pltpu.make_async_copy(
                out_piece(zz), ol_ref.at[z % 2, core], o_recv.at[z % 2, core]
            ).start()

        @pl.when(jnp.logical_not(out_here(zz)))
        def _():
            out_copy(zz).start()

    keep_probs = pltpu.make_async_copy(probs_ref, probs_hbm, id_sem.at[2])
    keep_probs.start()

    def backward(n, carry):
        grad_rows = da_ref[n]
        delta = jnp.sum(outs[n].astype(F32) * grad_rows.astype(F32), axis=1, keepdims=True)
        prob_grad = lax.dot_general(
            grad_rows, vcat[n], CONTRACT_LAST, preferred_element_type=F32
        )
        score_grad = (full[n] * (prob_grad - delta) * scale).astype(BF16)
        scores_ref[n] = score_grad
        dq_ref[n] = jnp.dot(score_grad, kcat[n], preferred_element_type=F32).astype(BF16)
        return carry

    for zz in range(4):
        arrive(da_ref.at[pl.ds(2 * zz, 2)], g_recv.at[zz], g_send.at[0, 0])
        if zz % 2 == 1:
            lax.fori_loop(2 * zz - 2, 2 * zz + 2, backward, 0, unroll=4)
    keep_scores = pltpu.make_async_copy(scores_ref, scores_hbm, id_sem.at[3])
    keep_scores.start()

    for j in (0, 1):
        for r in (0, 1):
            arrive(ol_ref.at[j, r], o_recv.at[j, r], o_send.at[0])
    for t in (0, 1):
        for args in kv_args(t):
            line_sent(*args)
        for args in grad_args(t):
            line_sent(*args)
    for args in query_args():
        line_sent(*args)
    for zz in range(4):

        @pl.when(jnp.logical_not(out_here(zz)))
        def _():
            out_copy(zz).wait_send()

    for copy in sent:
        copy.wait_send()
    keep_probs.wait()
    keep_scores.wait()


def gather(q, k, v, dm, w, random_blocks, global_blocks):
    vmem = pl.BlockSpec(memory_space=pltpu.VMEM)
    smem = pl.BlockSpec(memory_space=pltpu.SMEM)
    hbm = pl.BlockSpec(memory_space=pl.ANY)
    dma = pltpu.SemaphoreType.DMA
    blocks = jax.ShapeDtypeStruct((8, BLOCK, HEAD_DIM), BF16)
    weights = jax.ShapeDtypeStruct((8, BLOCK, SLOTS * BLOCK), BF16)
    return pl.pallas_call(
        gather_kernel,
        out_shape=(
            jax.ShapeDtypeStruct((4, 8, 128), jnp.int32),
            blocks,
            blocks,
            weights,
            weights,
            blocks,
            jax.ShapeDtypeStruct((2, 2, 2, BLOCK, HEAD_DIM), BF16),
        ),
        in_specs=[vmem] * 4 + [hbm] + [smem] * 2,
        out_specs=(vmem, vmem, vmem, hbm, hbm, vmem, vmem),
        scratch_shapes=[
            pltpu.VMEM((256, 4096), BF16),
            pltpu.VMEM((8, BLOCK, SLOTS * BLOCK), BF16),
            pltpu.VMEM((8, BLOCK, SLOTS * BLOCK), BF16),
            pltpu.VMEM((128, BLOCK, HEAD_DIM), BF16),
            pltpu.VMEM((8, 128), jnp.int32),
            pltpu.VMEM((2, 2, 4, 2, 256, 256), BF16),
            pltpu.VMEM((4, BLOCK, 256), BF16),
            pltpu.VMEM((256, 256), F32),
            pltpu.SMEM((4, 8, 128), jnp.int32),
            pltpu.VMEM((8, BLOCK, HEAD_DIM), BF16),
            pltpu.VMEM((8, BLOCK, SLOTS * BLOCK), F32),
            pltpu.VMEM((8, SLOTS * BLOCK, HEAD_DIM), BF16),
            pltpu.VMEM((8, SLOTS * BLOCK, HEAD_DIM), BF16),
            dma((4,)),
            dma((3, 2, 2)),
            dma((3, 4)),
            dma((3,)),
            dma((3,)),
            dma((2, 4)),
            dma((2, 4)),
            dma((2, 4)),
            dma((2, 4)),
            dma((2,)),
            dma((2,)),
            dma((2, 2, 3)),
            dma((2, 2, 3)),
            dma((2, 4, 2)),
            dma((2, 4, 2)),
            dma((2, 2)),
            dma((4,)),
            dma((4,)),
            dma((2, 2)),
        ],
        compiler_params=pltpu.CompilerParams(
            collective_id=0, has_side_effects=True, vmem_limit_bytes=VMEM_LIMIT
        ),
        name="gather_heads",
    )(q, k, v, dm, w, random_blocks, global_blocks)


def key_grads_kernel(
    ids_ref, q_ref, da_ref, probs_hbm, scores_hbm, dkv_hbm, acc, probs_ref, scores_ref, half, sems, out_sems
):
    core = place()[4]

    def load(part):
        rows = pl.ds(4 * part, 4)
        return (
            pltpu.make_async_copy(
                scores_hbm.at[rows], scores_ref.at[rows], sems.at[part, 0]
            ),
            pltpu.make_async_copy(probs_hbm.at[rows], probs_ref.at[rows], sems.at[part, 1]),
        )

    for part in (0, 1):
        for copy in load(part):
            copy.start()

    def clear(i, carry):
        acc[i] = jnp.zeros((BLOCK, HEAD_DIM), F32)
        return carry

    lax.fori_loop(0, 128, clear, 0, unroll=8)

    def one(n, carry):
        key_add = lax.dot_general(
            scores_ref[n], q_ref[n], CONTRACT_FIRST, preferred_element_type=F32
        )
        value_add = lax.dot_general(
            probs_ref[n], da_ref[n], CONTRACT_FIRST, preferred_element_type=F32
        )
        for t in range(SLOTS):
            at = ids_ref[n // 2, 2 * core + n % 2, t]
            acc[at] += key_add[t * BLOCK : (t + 1) * BLOCK, :]
            acc[at + 8] += value_add[t * BLOCK : (t + 1) * BLOCK, :]
        return carry

    for part in (0, 1):
        for copy in load(part):
            copy.wait()
        lax.fori_loop(4 * part, 4 * part + 4, one, 0, unroll=2)

    def store(part):
        rows = pl.ds(16 * part, 16)
        return pltpu.make_async_copy(half.at[rows], dkv_hbm.at[rows], out_sems.at[part])

    for part in range(8):

        def finish(i, carry):
            half[i] = acc[i].astype(BF16)
            return carry

        lax.fori_loop(16 * part, 16 * part + 16, finish, 0, unroll=8)
        store(part).start()
    for part in range(8):
        store(part).wait()


def key_grads(ids, q, da, probs, scores):
    vmem = pl.BlockSpec(memory_space=pltpu.VMEM)
    smem = pl.BlockSpec(memory_space=pltpu.SMEM)
    hbm = pl.BlockSpec(memory_space=pl.ANY)
    dma = pltpu.SemaphoreType.DMA
    return pl.pallas_call(
        key_grads_kernel,
        out_shape=jax.ShapeDtypeStruct((128, BLOCK, HEAD_DIM), BF16),
        in_specs=[smem, vmem, vmem, hbm, hbm],
        out_specs=hbm,
        scratch_shapes=[
            pltpu.VMEM((128, BLOCK, HEAD_DIM), F32),
            pltpu.VMEM((8, BLOCK, SLOTS * BLOCK), BF16),
            pltpu.VMEM((8, BLOCK, SLOTS * BLOCK), BF16),
            pltpu.VMEM((128, BLOCK, HEAD_DIM), BF16),
            dma((2, 2)),
            dma((8,)),
        ],
        compiler_params=pltpu.CompilerParams(vmem_limit_bytes=VMEM_LIMIT),
        name="key_grads",
    )(ids, q, da, probs, scores)


def unpack(pieces, out_ref):
    for j in (0, 1):
        for r in (0, 1):
            for low in (0, 1):
                row = (2 * r + low) * BLOCK
                out_ref[row : row + BLOCK, j * 128 : (j + 1) * 128] = pieces[j, r, low]


def scatter_kernel(
    ol_ref,
    dq_ref,
    p_hbm,
    w_hbm,
    mixed_ref,
    lands,
    w_ref,
    p_ref,
    load_sems,
    attn,
    terms,
    terms_in,
    xa,
    xc,
    total,
    zb,
    parts,
    parts_in,
    ya,
    yc,
    final,
    l_send,
    l_recv,
    ps_send,
    ps_recv,
    y_send,
    y_recv,
    xs_send,
    xs_recv,
    x_send,
    x_recv,
    z_send,
    z_recv,
):
    z, y, x, zh, core = place()
    sibling = dev(z, y, x, zh, 1 - core)
    sent = []
    load_w = pltpu.make_async_copy(w_hbm, w_ref, load_sems.at[0])
    load_p = pltpu.make_async_copy(p_hbm.at[:, core], p_ref, load_sems.at[1])
    load_w.start()
    load_p.start()
    unpack(ol_ref, attn)
    greet()

    def send(src, dst, send_sem, recv_sem, device):
        copy = copy_to(src, dst, send_sem, recv_sem, device)
        copy.start()
        sent.append(copy)

    def arrive(dst, recv_sem, send_sem):
        copy_to(dst, dst, send_sem, recv_sem, sibling).wait_recv()

    y_dev = (dev(z, (y + 1) % 4, x, zh, core), dev(z, (y + 3) % 4, x, zh, core))
    x_dev = (dev(z, y, (x + 1) % 4, zh, core), dev(z, y, (x + 3) % 4, zh, core))
    y_of = ((y + 2) % 4, (y + 1) % 4, (y + 3) % 4, y)
    x_of = ((x + 2) % 4, (x + 1) % 4, (x + 3) % 4, x)

    def back(u, zz, src):
        dst = lands.at[0, z % 2, core] if u == 0 else grad_land(u - 1, z % 2, core)
        return src, dst, l_send.at[u, zz], l_recv.at[u, z % 2, core], zz

    def start_back(src, dst, send_sem, recv_sem, zz):
        here = jnp.logical_and(z == zz, z // 2 == core)

        @pl.when(here)
        def _():
            pltpu.make_async_copy(src, dst, recv_sem).start()

        @pl.when(jnp.logical_not(here))
        def _():
            copy_to(src, dst, send_sem, recv_sem, dev(zz, y, x, zh, z // 2)).start()

    def sent_back(src, dst, send_sem, recv_sem, zz):
        here = jnp.logical_and(z == zz, z // 2 == core)

        @pl.when(jnp.logical_not(here))
        def _():
            copy_to(src, dst, send_sem, recv_sem, dev(zz, y, x, zh, z // 2)).wait_send()

    def landed(u):
        for j in (0, 1):
            for r in (0, 1):
                dst = lands.at[0, j, r] if u == 0 else grad_land(u - 1, j, r)
                arrive(dst, l_recv.at[u, j, r], l_send.at[u, 0])

    def grad_land(u, j, r):
        return lands.at[1 + u // 2, j, r, u % 2]

    def query_piece(zz):
        return dq_ref.at[pl.ds(2 * zz, 2)]

    def parts_to_sibling(t):
        for n in range(4):
            send(
                p_hbm.at[y_of[n], 1 - core, t // 2, :, t % 2],
                parts_in.at[t, n],
                ps_send.at[t, n],
                ps_recv.at[t, n],
                sibling,
            )

    def add_parts(t, n, zz, more):
        value = p_ref[y_of[n], t // 2, zz, t % 2].astype(F32) + parts_in[t, n, zz].astype(F32)
        for ref in more:
            value += ref.astype(F32)
        return value.astype(BF16)

    def parts_here(t, n):
        arrive(parts_in.at[t, n], ps_recv.at[t, n], ps_send.at[t, n])

    def parts_far(t):
        parts_here(t, 0)
        for side in (0, 1):
            for zz in (2 * side, 2 * side + 1):
                parts[t, 0, zz] = add_parts(t, 0, zz, ())
            send(
                parts.at[t, 0, pl.ds(2 * side, 2)],
                ya.at[t, side],
                y_send.at[t, side],
                y_recv.at[t, side],
                y_dev[side],
            )

    def parts_near(t):
        for side in (0, 1):
            n = 1 + side
            parts_here(t, n)
            for zz in (2 - 2 * side, 3 - 2 * side):
                parts[t, n, zz] = add_parts(t, n, zz, ())
            arrive(ya.at[t, side], y_recv.at[t, side], y_send.at[t, side])
            for low in (0, 1):
                zz = 2 * side + low
                parts[t, n, zz] = add_parts(t, n, zz, (ya[t, side, low],))
            send(
                parts.at[t, n],
                yc.at[t, side],
                y_send.at[t, n + 1],
                y_recv.at[t, n + 1],
                y_dev[side],
            )

    def parts_end(t):
        parts_here(t, 3)
        for side in (0, 1):
            arrive(yc.at[t, side], y_recv.at[t, 2 + side], y_send.at[t, 2 + side])
        for zz in range(4):
            final[t, zz] = add_parts(t, 3, zz, (yc[t, 0, zz], yc[t, 1, zz]))
            start_back(*back(1 + t, zz, final.at[t, zz]))

    def make_terms(wave, to_core, n):
        for k in (0, 1):
            at = pl.multiple_of((x_of[n] * 4 + k * 2 + to_core) * 256, 256)
            terms[wave, to_core, n, k] = jnp.dot(
                attn[wave * 128 : (wave + 1) * 128, :],
                w_ref[:, pl.ds(at, 256)],
                preferred_element_type=F32,
            ).astype(BF16)

    def terms_to_sibling(wave):
        for n in range(4):
            make_terms(wave, 1 - core, n)
            send(
                terms.at[wave, 1 - core, n],
                terms_in.at[wave, n],
                xs_send.at[wave, n],
                xs_recv.at[wave, n],
                sibling,
            )

    def terms_here(wave, n):
        make_terms(wave, core, n)
        arrive(terms_in.at[wave, n], xs_recv.at[wave, n], xs_send.at[wave, n])

    def add_terms(wave, n, k, more):
        value = terms[wave, core, n, k].astype(F32) + terms_in[wave, n, k].astype(F32)
        for ref in more:
            value += ref.astype(F32)
        return value.astype(BF16)

    def terms_far(wave):
        terms_here(wave, 0)
        for k in (0, 1):
            terms[wave, core, 0, k] = add_terms(wave, 0, k, ())
            send(
                terms.at[wave, core, 0, k],
                xa.at[wave, k],
                x_send.at[wave, k],
                x_recv.at[wave, k],
                x_dev[k],
            )

    def terms_near(wave):
        for side in (0, 1):
            n = 1 + side
            terms_here(wave, n)
            arrive(xa.at[wave, side], x_recv.at[wave, side], x_send.at[wave, side])
            terms[wave, core, n, side] = add_terms(wave, n, side, (xa[wave, side],))
            terms[wave, core, n, 1 - side] = add_terms(wave, n, 1 - side, ())
            send(
                terms.at[wave, core, n],
                xc.at[wave, side],
                x_send.at[wave, n + 1],
                x_recv.at[wave, n + 1],
                x_dev[side],
            )

    def terms_end(wave):
        terms_here(wave, 3)
        for side in (0, 1):
            arrive(xc.at[wave, side], x_recv.at[wave, 2 + side], x_send.at[wave, 2 + side])

        def add_total(k):
            total[wave, k] = add_terms(wave, 3, k, (xc[wave, 0, k], xc[wave, 1, k]))

        add_total(1 - zh)
        send(
            total.at[wave, 1 - zh],
            zb.at[wave],
            z_send.at[wave],
            z_recv.at[wave],
            dev(z, y, x, 1 - zh, core),
        )
        add_total(zh)

    def mixed_end(wave):
        arrive(zb.at[wave], z_recv.at[wave], z_send.at[wave])
        mixed_ref[wave * 128 : (wave + 1) * 128, :] = (
            total[wave, zh].astype(F32) + zb[wave].astype(F32)
        ).astype(BF16)

    parts_to_sibling(0)
    parts_to_sibling(1)
    for zz in range(4):
        start_back(*back(0, zz, query_piece(zz)))
    load_w.wait()
    terms_to_sibling(0)
    load_p.wait()
    parts_far(0)
    parts_to_sibling(2)
    terms_to_sibling(1)
    terms_far(0)
    parts_far(1)
    parts_to_sibling(3)
    terms_to_sibling(2)
    parts_near(0)
    terms_far(1)
    parts_far(2)
    terms_to_sibling(3)
    terms_near(0)
    parts_near(1)
    terms_far(2)
    parts_far(3)
    parts_end(0)
    terms_near(1)
    parts_near(2)
    terms_far(3)
    terms_end(0)
    parts_end(1)
    terms_near(2)
    parts_near(3)
    terms_end(1)
    parts_end(2)
    terms_near(3)
    terms_end(2)
    parts_end(3)
    terms_end(3)
    for wave in range(4):
        mixed_end(wave)
    for u in range(5):
        landed(u)
    for zz in range(4):
        sent_back(*back(0, zz, query_piece(zz)))
        for t in range(4):
            sent_back(*back(1 + t, zz, final.at[t, zz]))
    for copy in sent:
        copy.wait_send()


def scatter(ol, dq, dkv, w):
    vmem = pl.BlockSpec(memory_space=pltpu.VMEM)
    hbm = pl.BlockSpec(memory_space=pl.ANY)
    dma = pltpu.SemaphoreType.DMA
    return pl.pallas_call(
        scatter_kernel,
        out_shape=(
            jax.ShapeDtypeStruct((512, 256), BF16),
            jax.ShapeDtypeStruct((3, 2, 2, 2, BLOCK, HEAD_DIM), BF16),
        ),
        in_specs=[vmem, vmem, hbm, hbm],
        out_specs=(vmem,) * 2,
        scratch_shapes=[
            pltpu.VMEM((256, 4096), BF16),
            pltpu.VMEM((4, 2, 4, 2, BLOCK, HEAD_DIM), BF16),
            dma((2,)),
            pltpu.VMEM((512, 256), BF16),
            pltpu.VMEM((4, 2, 4, 2, 128, 256), BF16),
            pltpu.VMEM((4, 4, 2, 128, 256), BF16),
            pltpu.VMEM((4, 2, 128, 256), BF16),
            pltpu.VMEM((4, 2, 2, 128, 256), BF16),
            pltpu.VMEM((4, 2, 128, 256), BF16),
            pltpu.VMEM((4, 128, 256), BF16),
            pltpu.VMEM((4, 4, 4, BLOCK, HEAD_DIM), BF16),
            pltpu.VMEM((4, 4, 4, BLOCK, HEAD_DIM), BF16),
            pltpu.VMEM((4, 2, 2, BLOCK, HEAD_DIM), BF16),
            pltpu.VMEM((4, 2, 4, BLOCK, HEAD_DIM), BF16),
            pltpu.VMEM((4, 4, BLOCK, HEAD_DIM), BF16),
            dma((5, 4)),
            dma((5, 2, 2)),
            dma((4, 4)),
            dma((4, 4)),
            dma((4, 4)),
            dma((4, 4)),
            dma((4, 4)),
            dma((4, 4)),
            dma((4, 4)),
            dma((4, 4)),
            dma((4,)),
            dma((4,)),
        ],
        compiler_params=pltpu.CompilerParams(
            collective_id=1, has_side_effects=True, vmem_limit_bytes=VMEM_LIMIT
        ),
        name="scatter_heads",
    )(ol, dq, dkv, w)


def unpack_kernel(mixed_ref, lands_ref, mixed_out, dq_out, dk_out, dv_out):
    mixed_out[...] = mixed_ref[...]
    unpack(lands_ref.at[0], dq_out)
    unpack(lands_ref.at[1], dk_out)
    unpack(lands_ref.at[2], dv_out)


def unpack_all(mixed, lands):
    vmem = pl.BlockSpec(memory_space=pltpu.VMEM)
    return pl.pallas_call(
        unpack_kernel,
        out_shape=(jax.ShapeDtypeStruct((512, 256), BF16),) * 4,
        in_specs=[vmem] * 2,
        out_specs=(vmem,) * 4,
        name="unpack_outputs",
    )(mixed, lands)


def body(queries, keys, values, w_out, d_mixed, random_blocks, global_blocks):
    by_block = (4, BLOCK, 2 * HEAD_DIM)
    ids, q, da, probs, scores, dq, ol = gather(
        queries.reshape(by_block),
        keys.reshape(by_block),
        values.reshape(by_block),
        d_mixed,
        w_out,
        random_blocks,
        global_blocks,
    )
    dkv = key_grads(ids, q, da, probs, scores)
    dkv = dkv.reshape(4, 2, 2, 4, 2, BLOCK, HEAD_DIM)
    return unpack_all(*scatter(ol, dq, dkv, w_out))


def solution(mesh):
    return jax.shard_map(
        body,
        mesh=mesh,
        in_specs=(
            P("seq", "head"),
            P("seq", "head"),
            P("seq", "head"),
            P("head", None),
            P("seq", "head"),
            P("seq", None),
            P(),
        ),
        out_specs=(P("seq", "head"), P("seq", "head"), P("seq", "head"), P("seq", "head")),
        check_vma=False,
    )
```
